128 devices in a mesh: group: 8 (over x_lo, y), inner: 16 (over x_hi, z, core).
Axes of the slice: x: 4 (x_hi: 2, x_lo: 2; x = x_hi * 2 + x_lo), y: 4, z: 4, core: 2. Of those that a mesh axis runs over, the one named last changes fastest.
Arguments:
- visits: bfloat16 [65536, 1024], P(('group', 'inner')), may hold values from -6 to 6
- enc_weight: bfloat16 [1024, 1024], replicated, may hold values from -0.1875 to 0.1875
- drug_table: bfloat16 [4096, 1024], P(('group', 'inner')), may hold values from -0.59765625 to 0.59765625
- labels: int32 [65536, 32], P(('group', 'inner')), may hold values from 0 to 4095, as said below
- drug_order: int32 [4096], replicated, may hold values from 0 to 4095, each once
Outputs:
- drug_grad: float32 [4096, 1024], P(('group', 'inner'))
- weight_grad: float32 [1024, 1024], replicated
The draws below stay inside these ranges and needn't reach their ends.
Inputs may be any that keep to these rules, and one draw needn't show every extreme that they name: `labels`: each visit lists 32 different catalogue ids; the id in column j lies in [j * 128, (j + 1) * 128); every id of the window is listed by some visit. `drug_order`: A permutation of the catalogue ids.
All inputs are finite; a program needn't handle non-finite values.
Results may differ from the reference program's by a relative error of at most 0.00093.
Values may be sent and summed in bfloat16 or wider, within the bound.
A program may use at most 128 MiB of HBM per device.

```python
import math
import jax
import jax.numpy as jnp
from jax import lax

E = 1024
K = 32
V_DEV = 512
DRUGS = 4096
VISITS = 65536


def draw_labels(key, part):
    key = jax.random.fold_in(key, 7)
    block_width = DRUGS // K
    first_key, rest_key = jax.random.split(key)
    orders = jax.vmap(lambda sub: jax.random.permutation(sub, block_width))(jax.random.split(first_key, K))
    leading = jnp.transpose(orders).astype(jnp.int32)
    others = jax.random.randint(rest_key, (VISITS - block_width, K), 0, block_width, dtype=jnp.int32)
    inside = jnp.concatenate([leading, others], axis=0)
    offsets = (jnp.arange(K, dtype=jnp.int32) * block_width)[None, :]
    return (inside + offsets).astype(jnp.int32)


def block_levels(rng, dims, cuts, least, largest):
    def one(axis_at, shards_of):
        steps = jax.random.uniform(jax.random.fold_in(jax.random.fold_in(rng, 6), axis_at), (shards_of,), jnp.float32, least / len(cuts), largest / len(cuts))
        return jnp.repeat(jnp.exp(steps), dims[axis_at] // shards_of).reshape((-1,) + (1,) * (len(dims) - axis_at - 1))

    factor_of = one(*cuts[0])
    for cut in cuts[1:]:
        factor_of = factor_of * one(*cut)
    return factor_of


def centred(own_key, extent, spread, reach, pieces=(), kind=jnp.bfloat16):
    gain = block_levels(own_key, extent, pieces, -0.22, 0.18) if pieces else 1.0
    values = jax.random.normal(own_key, extent, jnp.float32) * spread * gain
    return jnp.minimum(jnp.maximum(values, -reach), reach).astype(kind)


def setup_inputs(seed: int = 0) -> dict:
    arg_keys = jax.random.split(jax.random.key(seed), 6)
    visits = centred(arg_keys[0], (VISITS, E), 1.0, 6.0, ((0, 128),))
    enc_weight = centred(arg_keys[1], (E, E), E ** -0.5, 0.1875)
    drug_table = centred(arg_keys[2], (DRUGS, E), 0.1, 0.59765625, ((0, 128),))
    labels = draw_labels(jax.random.fold_in(arg_keys[5], 71), 0)
    drug_order = jax.random.permutation(arg_keys[4], DRUGS).astype(jnp.int32)
    return dict(visits=visits, enc_weight=enc_weight, drug_table=drug_table, labels=labels, drug_order=drug_order)


def targets(block_labels, inverse, drug_count):
    ranks = inverse[block_labels]
    positions = jnp.arange(block_labels.shape[0], dtype=jnp.int32)[:, None]
    return jnp.zeros((block_labels.shape[0], drug_count), jnp.bfloat16).at[positions, ranks].set(1.0)

def reference(visits, enc_weight, drug_table, labels, drug_order):
    drug_count = drug_table.shape[0]
    inverse = jnp.zeros((drug_count,), jnp.int32).at[drug_order].set(jnp.arange(drug_count, dtype=jnp.int32))
    loss_scale = 1.0 / math.sqrt(visits.shape[0])
    blocks = visits.shape[0] // V_DEV

    def advance(carry, index):
        drug_grad, weight_grad = carry
        offset = (index * V_DEV).astype(jnp.int32)
        block_rows = lax.dynamic_slice_in_dim(visits, offset, V_DEV, 0)
        block_labels = lax.dynamic_slice_in_dim(labels, offset, V_DEV, 0)
        hidden = jnp.dot(block_rows, enc_weight, preferred_element_type=jnp.float32)
        squash = jnp.tanh(hidden)
        coded = squash.astype(jnp.bfloat16)
        labelled = targets(block_labels, inverse, drug_count).astype(jnp.float32)
        logits = lax.dot_general(coded, drug_table, (((1,), (1,)), ((), ())), preferred_element_type=jnp.float32)
        residual = (loss_scale * (jax.nn.sigmoid(logits) - labelled)).astype(jnp.bfloat16)
        term = lax.dot_general(residual, coded, (((0,), (0,)), ((), ())), preferred_element_type=jnp.float32)
        term = lax.optimization_barrier(term.astype(jnp.bfloat16))
        coded_grad = jnp.dot(residual, drug_table, preferred_element_type=jnp.float32)
        hidden_grad = (coded_grad * (1.0 - squash * squash)).astype(jnp.bfloat16)
        weight_part = lax.dot_general(block_rows, hidden_grad, (((0,), (0,)), ((), ())), preferred_element_type=jnp.float32)
        return ((drug_grad + term.astype(jnp.float32), weight_grad + weight_part), None)
    start_state = (jnp.zeros(drug_table.shape, jnp.float32), jnp.zeros(enc_weight.shape, jnp.float32))
    (drug_grad, weight_grad), _ = lax.scan(advance, start_state, jnp.arange(blocks, dtype=jnp.int32))
    return (drug_grad, weight_grad)
```

```python
import math

import jax
import jax.numpy as jnp
from jax import lax
from jax.experimental import pallas as pl
from jax.experimental.pallas import tpu as pltpu
from jax.sharding import PartitionSpec as P

MESH = pl.DeviceIdType.MESH
F32 = jnp.float32
BF16 = jnp.bfloat16
NN = (((1,), (0,)), ((), ()))
NT = (((1,), (1,)), ((), ()))

PARTS = ((0, 1, 2), (1, 2, 0), (2, 0, 1))
COLS = ((0, 384), (384, 384), (768, 256))
OFFS = (1, -1, 2)
REL = (0, 1, -1, 2)


def mod4(v):
    return lax.rem(v + 8, 4)


def kernel(
    visits, weight, table, labels, order, dgrad, wgrad,
    vis, vis_t, w_half, w_t, own_order, own_labels, order_t, sel, lab, coded, squash, tab, tab_t, res,
    cg_out, cg_in, cg_own, hgrad,
    s0, s1, s2, fp0, fp1, fp2, own0, own1, own2, hb0, hb1, hb2, rb0, rb1, rb2, r2b0, r2b1, r2b2, r2s0, r2s1, r2s2,
    r3b0, r3b1, r3b2,
    wfull, wlow, w1b0, w1b1, w1b2, wp0, wp1, wp2, w2b0, w2b1, w2b2, wq0, wq1, wq2, w3b0, w3b1, w3b2, wout,
    load_sem, ag_s, ag_r, rs_s, rs_r, wt_s, wt_r, d2d_s, d2d_r, out_l, out_s, out_r,
):
    g, i = lax.axis_index("group"), lax.axis_index("inner")
    x = (i // 8) * 2 + g // 4
    y = lax.rem(g, 4)
    z = lax.rem(i // 2, 4)
    core = lax.rem(i, 2)
    pos = (x, y, z)

    def device(px, py, pz, pc):
        return (lax.rem(px, 2) * 4 + py, (px // 2) * 8 + pz * 2 + pc)

    def peer(axis, off):
        moved = [mod4(v + off) if k == axis else v for k, v in enumerate(pos)]
        return device(*moved, core)

    sibling = device(x, y, z, 1 - core)
    sends = []

    def send(src, dst, ssem, rsem, to):
        copy = pltpu.make_async_remote_copy(
            src_ref=src, dst_ref=dst, send_sem=ssem, recv_sem=rsem, device_id=to, device_id_type=MESH
        )
        copy.start()
        sends.append(copy)

    def received(dst, ssem, rsem, to):
        pltpu.make_async_remote_copy(
            src_ref=dst, dst_ref=dst, send_sem=ssem, recv_sem=rsem, device_id=to, device_id_type=MESH
        ).wait_recv()

    def cols(p):
        return pl.ds(COLS[p][0], COLS[p][1])

    def row_of(buf, p, b_at, c_at):
        a, b, c = PARTS[p]
        at = [None, None, None]
        at[a], at[b], at[c] = slice(None), b_at, c_at
        return buf.at[at[2], at[1], at[0], :, cols(p)]

    def block_of(buf, p, a_at, b_at, c_at):
        a, b, c = PARTS[p]
        at = [None, None, None]
        at[a], at[b], at[c] = a_at, b_at, c_at
        return buf.at[at[2], at[1], at[0], :, cols(p)]

    def plane_row(buf, p, b_at):
        return buf.at[:, b_at] if p == 2 else buf.at[b_at]

    mine = pl.ds(pl.multiple_of(core * 512, 512), 512)
    theirs = pl.ds(pl.multiple_of((1 - core) * 512, 512), 512)
    loads = [
        pltpu.make_async_copy(table, tab.at[z, y, x], load_sem.at[0]),
        pltpu.make_async_copy(weight.at[:, mine], w_half, load_sem.at[1]),
        pltpu.make_async_copy(visits, vis.at[mine], load_sem.at[2]),
        pltpu.make_async_copy(labels, own_labels, load_sem.at[3]),
        pltpu.make_async_copy(order, own_order, load_sem.at[4]),
    ]
    for load in loads:
        load.start()
    barrier = pltpu.get_barrier_semaphore()
    partners = [peer(axis, off) for axis in range(3) for off in OFFS] + [sibling]
    for partner in partners:
        pl.semaphore_signal(barrier, inc=1, device_id=partner, device_id_type=MESH)
    pl.semaphore_wait(barrier, len(partners))

    for k, off in enumerate(OFFS):
        for p in range(3):
            a, b, c = PARTS[p]
            send(table.at[:, cols(p)], block_of(tab, p, pos[a], pos[b], pos[c]), ag_s.at[p, k], ag_r.at[p, k], peer(a, off))
    send(visits, vis.at[mine], d2d_s.at[0], d2d_r.at[0], sibling)

    loads[3].wait()
    lane = lax.broadcasted_iota(jnp.int32, (512, 32), 1)
    lab[mine, :] = jnp.concatenate(
        [
            (own_labels[...] - lane * 128).astype(F32),
            jnp.ones((512, 1), F32),
            jnp.zeros((512, 95), F32),
        ],
        axis=1,
    ).astype(BF16)
    send(lab.at[mine], lab.at[mine], d2d_s.at[1], d2d_r.at[1], sibling)
    loads[1].wait()
    w_t[...] = w_half[...].T
    loads[0].wait()
    for p in range(3):
        a, b, c = PARTS[p]
        for k, off in enumerate(OFFS):
            received(block_of(tab, p, mod4(pos[a] - off), pos[b], pos[c]), ag_s.at[p, k], ag_r.at[p, k], peer(a, off))

    def send_row_c(p, j, b_at):
        a, b, c = PARTS[p]
        row = row_of(tab, p, b_at, pos[c])
        for d, off in enumerate((1, -1)):
            send(row, row, ag_s.at[p, 6 + 2 * j + d], ag_r.at[p, 6 + 2 * j + d], peer(c, off))

    for p in range(3):
        a, b, c = PARTS[p]
        row = row_of(tab, p, pos[b], pos[c])
        for k, off in enumerate(OFFS):
            send(row, row, ag_s.at[p, 3 + k], ag_r.at[p, 3 + k], peer(b, off))
        send_row_c(p, 0, pos[b])

    def hidden_of(rows):
        hidden = lax.dot_general(w_t[...], vis[rows, :], NT, preferred_element_type=F32)
        value = jnp.tanh(hidden)
        squash[:, rows] = value
        coded[mine, rows] = value.astype(BF16)

    loads[2].wait()
    hidden_of(mine)

    for k, off in enumerate(OFFS):
        for p in range(3):
            a, b, c = PARTS[p]
            b_at = mod4(pos[b] - off)
            received(row_of(tab, p, b_at, pos[c]), ag_s.at[p, 3 + k], ag_r.at[p, 3 + k], peer(b, off))
            send_row_c(p, REL.index(-off if off != 2 else 2), b_at)

    received(vis.at[theirs], d2d_s.at[0], d2d_r.at[0], sibling)
    hidden_of(theirs)
    send(coded.at[mine], coded.at[mine], d2d_s.at[2], d2d_r.at[2], sibling)

    def take_row(j):
        for p in range(3):
            a, b, c = PARTS[p]
            b_at = mod4(pos[b] + REL[j])
            low = row_of(tab, p, b_at, mod4(pos[c] - 1))
            received(low, ag_s.at[p, 6 + 2 * j], ag_r.at[p, 6 + 2 * j], peer(c, 1))
            if j in (0, 1):
                send(low, low, ag_s.at[p, 14 + j], ag_r.at[p, 14 + j], peer(c, 1))
            high = row_of(tab, p, b_at, mod4(pos[c] + 1))
            received(high, ag_s.at[p, 7 + 2 * j], ag_r.at[p, 7 + 2 * j], peer(c, -1))
            if j in (2, 3):
                send(high, high, ag_s.at[p, 14 + j], ag_r.at[p, 14 + j], peer(c, -1))

    take_row(0)
    loads[4].wait()
    order_t[...] = own_order[...].astype(F32).T
    lane_q = lax.broadcasted_iota(jnp.int32, (32, 32), 1)
    lane_j = lax.broadcasted_iota(jnp.int32, (32, 128), 1)

    def select(n, _):
        bz, by, bx = n // 16, lax.rem(n // 4, 4), lax.rem(n, 4)
        q = (lax.rem(bx, 2) * 4 + by) * 4 + (bx // 2) * 2 + bz // 2
        m = lax.rem(bz, 2) * 2 + core
        rows = order_t[pl.ds(pl.multiple_of(m * 32, 32), 32), :]
        ids = jnp.sum(jnp.where(lane_q == q, rows, 0.0), axis=1, keepdims=True).astype(jnp.int32)
        ids = jnp.broadcast_to(ids, (32, 128))
        picked = jnp.where(lane_j == (ids >> 7), 1.0, 0.0)
        sel[n] = jnp.where(lane_j == 32, -(ids & 127).astype(F32), picked).astype(BF16)
        return 0

    lax.fori_loop(0, 64, select, 0)
    take_row(2)
    vis_t[...] = vis[...].T
    take_row(1)
    take_row(3)
    received(coded.at[theirs], d2d_s.at[2], d2d_r.at[2], sibling)
    received(lab.at[theirs], d2d_s.at[1], d2d_r.at[1], sibling)
    for j in (0, 1, 2, 3):
        for p in range(3):
            a, b, c = PARTS[p]
            row = row_of(tab, p, mod4(pos[b] + REL[j]), mod4(pos[c] + 2))
            received(row, ag_s.at[p, 14 + j], ag_r.at[p, 14 + j], peer(c, 1 if j < 2 else -1))

    scale = 1.0 / 256.0

    def residual_of(n, _):
        plane, half = n // 2, lax.rem(n, 2)
        seen = pl.ds(pl.multiple_of(half * 512, 512), 512)
        rows = tab[plane].reshape(512, 1024)
        logits = lax.dot_general(rows, coded[:, seen], NN, preferred_element_type=F32)
        gap = lax.dot_general(
            sel[pl.ds(plane * 16, 16)].reshape(512, 128), lab[seen, :], NT, preferred_element_type=F32
        )
        prob = 0.5 * jnp.tanh(0.5 * logits) + 0.5
        value = (prob - jnp.where(gap == 0.0, 1.0, 0.0)) * scale
        res[plane, :, :, :, seen] = value.astype(BF16).reshape(4, 4, 32, 512)
        return 0

    lax.fori_loop(0, 8, residual_of, 0)

    s, fp, own = (s0, s1, s2), (fp0, fp1, fp2), (own0, own1, own2)
    hb, rb = (hb0, hb1, hb2), (rb0, rb1, rb2)
    r2b, r2s, r3b = (r2b0, r2b1, r2b2), (r2s0, r2s1, r2s2), (r3b0, r3b1, r3b2)

    def term(p, off):
        c_at = mod4(pos[PARTS[p][2]] + off)
        rows = (res[c_at], res[:, :, c_at], res[:, c_at])[p].reshape(512, 1024)
        value = lax.dot_general(rows, coded[cols(p), :], NT, preferred_element_type=F32)
        return value.reshape(4, 4, 32, COLS[p][1])

    for p in range(3):
        a, b, c = PARTS[p]
        s[p][2] = term(p, 2).astype(BF16)
        for j in range(4):
            src = plane_row(s[p].at[2], p, mod4(pos[b] + REL[j]))
            send(src, hb[p].at[j], rs_s.at[p, j], rs_r.at[p, j], peer(c, 1 if j < 2 else -1))

    def send_term_row(p, k, j):
        b, c = PARTS[p][1], PARTS[p][2]
        src = plane_row(s[p].at[k], p, mod4(pos[b] + REL[j]))
        send(src, rb[p].at[k, j], rs_s.at[p, 4 + 4 * k + j], rs_r.at[p, 4 + 4 * k + j], peer(c, OFFS[k]))

    for k in range(2):
        for p in range(3):
            a, b, c = PARTS[p]
            value = term(p, OFFS[k])
            fp[p][k] = value
            s[p][k] = value.astype(BF16)
            for j in (2, 3) if k == 0 else (0, 1):
                send_term_row(p, k, j)
    for p in range(3):
        own[p][...] = term(p, 0)

    for j in (0, 2, 1, 3):
        k = 0 if j < 2 else 1
        for p in range(3):
            a, b, c = PARTS[p]
            received(hb[p].at[j], rs_s.at[p, j], rs_r.at[p, j], peer(c, 1 if j < 2 else -1))
            b_at = mod4(pos[b] + REL[j])
            whole = plane_row(fp[p].at[k], p, b_at)[...] + hb[p][j].astype(F32)
            plane_row(s[p].at[k], p, b_at)[...] = whole.astype(BF16)
            send_term_row(p, k, j)

    def transposed(n, _):
        tab_t[:, pl.ds(pl.multiple_of(n * 512, 512), 512)] = tab[n].reshape(512, 1024).T
        return 0

    lax.fori_loop(0, 4, transposed, 0)
    flat = res.reshape(2048, 1024)

    def coded_grad(at):
        rows = tab_t[pl.ds(pl.multiple_of(at, 128), 128), :]
        return lax.dot_general(rows, flat[...], NN, preferred_element_type=F32)

    def away(n, _):
        cg_out[pl.ds(pl.multiple_of(n * 128, 128), 128), :] = coded_grad((1 - core) * 512 + n * 128).astype(BF16)
        return 0

    lax.fori_loop(0, 4, away, 0)
    send(cg_out, cg_in, d2d_s.at[3], d2d_r.at[3], sibling)

    def home(n, _):
        cg_own[pl.ds(pl.multiple_of(n * 128, 128), 128), :] = coded_grad(core * 512 + n * 128)
        return 0

    lax.fori_loop(0, 4, home, 0)
    received(cg_in, d2d_s.at[3], d2d_r.at[3], sibling)
    hgrad[...] = ((cg_own[...] + cg_in[...].astype(F32)) * (1.0 - squash[...] * squash[...])).astype(BF16)

    for half in range(2):
        value = lax.dot_general(vis_t[pl.ds(half * 512, 512), :], hgrad[...], NT, preferred_element_type=F32)
        wfull[:, pl.ds(half * 512, 512)] = value
        wlow[:, pl.ds(half * 512, 512)] = value.astype(BF16)
    w1b, wp, w2b, wq, w3b = (
        (w1b0, w1b1, w1b2), (wp0, wp1, wp2), (w2b0, w2b1, w2b2), (wq0, wq1, wq2), (w3b0, w3b1, w3b2)
    )

    def span(at, size):
        return pl.ds(pl.multiple_of(at * size, size), size)

    for k, off in enumerate(OFFS):
        for p in range(3):
            c = PARTS[p][2]
            src = wlow.at[span(mod4(pos[c] + off), 128), cols(p)]
            send(src, w1b[p].at[k], wt_s.at[p, k], wt_r.at[p, k], peer(c, off))

    for p in range(3):
        a, b, c = PARTS[p]
        for j in (2, 0, 1, 3):
            for k in range(2):
                received(rb[p].at[k, j], rs_s.at[p, 4 + 4 * k + j], rs_r.at[p, 4 + 4 * k + j], peer(c, OFFS[k]))
            mine_row = plane_row(own[p], p, mod4(pos[b] + REL[j]))
            mine_row[...] = mine_row[...] + rb[p][0, j].astype(F32) + rb[p][1, j].astype(F32)
        for k, off in enumerate(OFFS):
            src = plane_row(own[p], p, mod4(pos[b] + off))
            send(src, r2b[p].at[k], rs_s.at[p, 12 + k], rs_r.at[p, 12 + k], peer(b, off))

    for p in range(3):
        c = PARTS[p][2]
        for k, off in enumerate(OFFS):
            received(w1b[p].at[k], wt_s.at[p, k], wt_r.at[p, k], peer(c, off))
        wp[p][...] = (
            wfull[span(pos[c], 128), cols(p)]
            + w1b[p][0].astype(F32) + w1b[p][1].astype(F32) + w1b[p][2].astype(F32)
        )
        b = PARTS[p][1]
        for k, off in enumerate(OFFS):
            src = wp[p].at[span(mod4(pos[b] + off), 32)]
            send(src, w2b[p].at[k], wt_s.at[p, 3 + k], wt_r.at[p, 3 + k], peer(b, off))

    for p in range(3):
        a, b, c = PARTS[p]
        for k, off in enumerate(OFFS):
            received(r2b[p].at[k], rs_s.at[p, 12 + k], rs_r.at[p, 12 + k], peer(b, off))
        r2s[p][...] = plane_row(own[p], p, pos[b])[...] + r2b[p][0] + r2b[p][1] + r2b[p][2]
        for k, off in enumerate(OFFS):
            send(r2s[p].at[mod4(pos[a] + off)], r3b[p].at[k], rs_s.at[p, 15 + k], rs_r.at[p, 15 + k], peer(a, off))

    for p in range(3):
        a, b, c = PARTS[p]
        for k, off in enumerate(OFFS):
            received(w2b[p].at[k], wt_s.at[p, 3 + k], wt_r.at[p, 3 + k], peer(b, off))
        wq[p][...] = wp[p][span(pos[b], 32), :] + w2b[p][0] + w2b[p][1] + w2b[p][2]
        for k, off in enumerate(OFFS):
            src = wq[p].at[span(mod4(pos[a] + off), 8)]
            send(src, w3b[p].at[k], wt_s.at[p, 6 + k], wt_r.at[p, 6 + k], peer(a, off))

    for p in range(3):
        a, b, c = PARTS[p]
        for k, off in enumerate(OFFS):
            received(w3b[p].at[k], wt_s.at[p, 6 + k], wt_r.at[p, 6 + k], peer(a, off))
        at = span((pos[c] * 4 + pos[b]) * 4 + pos[a], 8)
        wout[at, cols(p)] = wq[p][span(pos[a], 8), :] + w3b[p][0] + w3b[p][1] + w3b[p][2]
        for k, off in enumerate(OFFS):
            block = wout.at[at, cols(p)]
            send(block, block, wt_s.at[p, 9 + k], wt_r.at[p, 9 + k], peer(a, off))

    for p in range(3):
        a, b, c = PARTS[p]
        for k, off in enumerate(OFFS):
            received(r3b[p].at[k], rs_s.at[p, 15 + k], rs_r.at[p, 15 + k], peer(a, off))
        dgrad[:, cols(p)] = r2s[p][pos[a]] + r3b[p][0] + r3b[p][1] + r3b[p][2]

    for p in range(3):
        a, b, c = PARTS[p]
        for k, off in enumerate(OFFS):
            block = wout.at[span((pos[c] * 4 + pos[b]) * 4 + mod4(pos[a] - off), 8), cols(p)]
            received(block, wt_s.at[p, 9 + k], wt_r.at[p, 9 + k], peer(a, off))
        for k, off in enumerate(OFFS):
            row = wout.at[span(pos[c] * 4 + pos[b], 32), cols(p)]
            send(row, row, wt_s.at[p, 12 + k], wt_r.at[p, 12 + k], peer(b, off))

    pieces = (((0, 0, 0, 384),), ((1, 384, 0, 128), (2, 512, 1, 256)), ((3, 768, 1, 256),))
    locals_ = []

    def deliver(p, n, c_at):
        for q, lo, half, size in pieces[p]:
            src = wout.at[span(c_at, 128), pl.ds(lo, size)]
            dst = wgrad.at[
                pl.ds(pl.multiple_of(half * 512 + c_at * 128, 128), 128),
                pl.ds(pl.multiple_of(core * 512 + lo - half * 512, 128), size),
            ]
            copy = pltpu.make_async_copy(src, dst, out_l.at[q, n])
            copy.start()
            locals_.append(copy)
            send(src, dst, out_s.at[q, n], out_r.at[q, n], sibling)

    for p in range(3):
        a, b, c = PARTS[p]
        for k, off in enumerate(OFFS):
            row = wout.at[span(pos[c] * 4 + mod4(pos[b] - off), 32), cols(p)]
            received(row, wt_s.at[p, 12 + k], wt_r.at[p, 12 + k], peer(b, off))
        plane = wout.at[span(pos[c], 128), cols(p)]
        for k, off in enumerate((1, -1)):
            send(plane, plane, wt_s.at[p, 15 + k], wt_r.at[p, 15 + k], peer(c, off))
        deliver(p, 0, pos[c])
    for p in range(3):
        c = PARTS[p][2]
        for k, off in enumerate((1, -1)):
            at = mod4(pos[c] - off)
            received(wout.at[span(at, 128), cols(p)], wt_s.at[p, 15 + k], wt_r.at[p, 15 + k], peer(c, off))
            half = wout.at[span(at * 2 + k, 64), cols(p)]
            send(half, half, wt_s.at[p, 17 + k], wt_r.at[p, 17 + k], peer(c, off))
            deliver(p, 1 + k, at)
    for p in range(3):
        c = PARTS[p][2]
        at = mod4(pos[c] + 2)
        for k, off in enumerate((1, -1)):
            received(wout.at[span(at * 2 + k, 64), cols(p)], wt_s.at[p, 17 + k], wt_r.at[p, 17 + k], peer(c, off))
        deliver(p, 3, at)
    for p in range(3):
        c = PARTS[p][2]
        for n, off in enumerate((0, -1, 1, 2)):
            c_at = mod4(pos[c] + off)
            for q, lo, half, size in pieces[p]:
                dst = wgrad.at[
                    pl.ds(pl.multiple_of(half * 512 + c_at * 128, 128), 128),
                    pl.ds(pl.multiple_of((1 - core) * 512 + lo - half * 512, 128), size),
                ]
                received(dst, out_s.at[q, n], out_r.at[q, n], sibling)
    for copy in sends:
        copy.wait_send()
    for copy in locals_:
        copy.wait()


def per_part(make):
    return [make(width) for _, width in COLS]


def local(visits, enc_weight, drug_table, labels, drug_order):
    vmem = pltpu.VMEM
    scratch = [
        vmem((1024, 1024), BF16), vmem((1024, 1024), BF16), vmem((1024, 512), BF16), vmem((512, 1024), BF16),
        vmem((32, 128), jnp.int32), vmem((512, 32), jnp.int32), vmem((128, 32), F32),
        vmem((64, 32, 128), BF16), vmem((1024, 128), BF16), vmem((1024, 1024), BF16), vmem((512, 1024), F32),
        vmem((4, 4, 4, 32, 1024), BF16), vmem((1024, 2048), BF16), vmem((4, 4, 4, 32, 1024), BF16),
        vmem((512, 1024), BF16), vmem((512, 1024), BF16), vmem((512, 1024), F32), vmem((512, 1024), BF16),
        *per_part(lambda n: vmem((3, 4, 4, 32, n), BF16)),
        *per_part(lambda n: vmem((2, 4, 4, 32, n), F32)),
        *per_part(lambda n: vmem((4, 4, 32, n), F32)),
        *per_part(lambda n: vmem((4, 4, 32, n), BF16)),
        *per_part(lambda n: vmem((2, 4, 4, 32, n), BF16)),
        *per_part(lambda n: vmem((3, 4, 32, n), F32)),
        *per_part(lambda n: vmem((4, 32, n), F32)),
        *per_part(lambda n: vmem((3, 32, n), F32)),
        vmem((512, 1024), F32), vmem((512, 1024), BF16),
        *per_part(lambda n: vmem((3, 128, n), BF16)),
        *per_part(lambda n: vmem((128, n), F32)),
        *per_part(lambda n: vmem((3, 32, n), F32)),
        *per_part(lambda n: vmem((32, n), F32)),
        *per_part(lambda n: vmem((3, 8, n), F32)),
        vmem((512, 1024), F32),
        pltpu.SemaphoreType.DMA((5,)),
        pltpu.SemaphoreType.DMA((3, 18)), pltpu.SemaphoreType.DMA((3, 18)),
        pltpu.SemaphoreType.DMA((3, 18)), pltpu.SemaphoreType.DMA((3, 18)),
        pltpu.SemaphoreType.DMA((3, 19)), pltpu.SemaphoreType.DMA((3, 19)),
        pltpu.SemaphoreType.DMA((4,)), pltpu.SemaphoreType.DMA((4,)),
        pltpu.SemaphoreType.DMA((4, 4)), pltpu.SemaphoreType.DMA((4, 4)), pltpu.SemaphoreType.DMA((4, 4)),
    ]
    anywhere = pl.BlockSpec(memory_space=pl.ANY)
    return pl.pallas_call(
        kernel,
        name="step",
        out_shape=(jax.ShapeDtypeStruct((32, 1024), F32), jax.ShapeDtypeStruct((1024, 1024), F32)),
        in_specs=[anywhere] * 5,
        out_specs=(pl.BlockSpec(memory_space=pltpu.VMEM), anywhere),
        scratch_shapes=scratch,
        compiler_params=pltpu.CompilerParams(
            collective_id=0, has_side_effects=True, vmem_limit_bytes=60 * 2**20
        ),
    )(visits, enc_weight, drug_table, labels, drug_order.reshape(32, 128))


def solution(mesh):
    return jax.shard_map(
        local,
        mesh=mesh,
        in_specs=(
            P(("group", "inner"), None),
            P(),
            P(("group", "inner"), None),
            P(("group", "inner"), None),
            P(),
        ),
        out_specs=(P(("group", "inner"), None), P()),
        check_vma=False,
    )
```

```python
import math

import jax
import jax.numpy as jnp
from jax import lax
from jax.experimental import pallas as pl
from jax.experimental.pallas import tpu as pltpu
from jax.sharding import PartitionSpec as P

MESH = pl.DeviceIdType.MESH
F32 = jnp.float32
BF16 = jnp.bfloat16
NN = (((1,), (0,)), ((), ()))
NT = (((1,), (1,)), ((), ()))

PARTS = ((0, 1, 2), (2, 1, 0), (2, 0, 1))
COLS = ((0, 384), (384, 384), (768, 256))
OFFS = (1, -1, 2)
REL = (0, 1, -1, 2)


def mod4(v):
    return lax.rem(v + 8, 4)


def kernel(
    visits, weight, table, labels, order, dgrad, wgrad,
    vis, vis_t, w_half, w_t, own_order, own_labels, order_t, sel, lab, coded, squash, tab, tab_t, res,
    cg_out, cg_in, cg_own, hgrad,
    s0, s1, s2, fp0, fp1, fp2, own0, own1, own2, hb0, hb1, hb2, rb0, rb1, rb2,
    r2a0, r2a1, r2a2, r2b0, r2b1, r2b2, r2s0, r2s1, r2s2,
    r3b0, r3b1, r3b2,
    wfull, wlow, w1b0, w1b1, w1b2, wp0, wp1, wp2, w2b0, w2b1, w2b2, wq0, wq1, wq2, w3b0, w3b1, w3b2, wout,
    load_sem, ag_s, ag_r, rs_s, rs_r, wt_s, wt_r, d2d_s, d2d_r, out_sem,
):
    g, i = lax.axis_index("group"), lax.axis_index("inner")
    x = (i // 8) * 2 + g // 4
    y = lax.rem(g, 4)
    z = lax.rem(i // 2, 4)
    core = lax.rem(i, 2)
    pos = (x, y, z)

    def device(px, py, pz, pc):
        return (lax.rem(px, 2) * 4 + py, (px // 2) * 8 + pz * 2 + pc)

    def peer(axis, off):
        moved = [mod4(v + off) if k == axis else v for k, v in enumerate(pos)]
        return device(*moved, core)

    sibling = device(x, y, z, 1 - core)
    def send(src, dst, ssem, rsem, to):
        copy = pltpu.make_async_remote_copy(
            src_ref=src, dst_ref=dst, send_sem=ssem, recv_sem=rsem, device_id=to, device_id_type=MESH
        )
        copy.start()

    def received(dst, rsem):
        pltpu.make_async_copy(dst, dst, rsem).wait()

    def cols(p):
        return pl.ds(COLS[p][0], COLS[p][1])

    def row_of(buf, p, b_at, c_at):
        a, b, c = PARTS[p]
        at = [None, None, None]
        at[a], at[b], at[c] = slice(None), b_at, c_at
        return buf.at[at[2], at[1], at[0], :, cols(p)]

    def block_of(buf, p, a_at, b_at, c_at):
        a, b, c = PARTS[p]
        at = [None, None, None]
        at[a], at[b], at[c] = a_at, b_at, c_at
        return buf.at[at[2], at[1], at[0], :, cols(p)]

    def plane_row(buf, p, b_at):
        return buf.at[b_at] if p == 0 else buf.at[:, b_at]

    mine = pl.ds(pl.multiple_of(core * 512, 512), 512)
    theirs = pl.ds(pl.multiple_of((1 - core) * 512, 512), 512)
    loads = [
        pltpu.make_async_copy(table, tab.at[z, y, x], load_sem.at[0]),
        pltpu.make_async_copy(weight.at[:, mine], w_half, load_sem.at[1]),
        pltpu.make_async_copy(visits, vis.at[mine], load_sem.at[2]),
        pltpu.make_async_copy(labels, own_labels, load_sem.at[3]),
        pltpu.make_async_copy(order, own_order, load_sem.at[4]),
    ]
    for load in loads:
        load.start()
    barrier = pltpu.get_barrier_semaphore()
    partners = [peer(axis, off) for axis in range(3) for off in OFFS] + [sibling]
    for partner in partners:
        pl.semaphore_signal(barrier, inc=1, device_id=partner, device_id_type=MESH)
    pl.semaphore_wait(barrier, len(partners))

    for k, off in enumerate(OFFS):
        for p in range(3):
            a, b, c = PARTS[p]
            send(table.at[:, cols(p)], block_of(tab, p, pos[a], pos[b], pos[c]), ag_s.at[p], ag_r.at[p, 15], peer(a, off))
    send(visits, vis.at[mine], d2d_s.at[0], d2d_r.at[0], sibling)

    loads[3].wait()
    column = lax.broadcasted_iota(jnp.int32, (32, 512), 0)
    ids_in_range = (own_labels[...] - column * 128).astype(F32)
    lab[mine, :] = jnp.concatenate([ids_in_range, jnp.ones((1, 512), F32), jnp.zeros((95, 512), F32)], axis=0).T.astype(BF16)
    send(lab.at[mine], lab.at[mine], d2d_s.at[1], d2d_r.at[1], sibling)
    loads[1].wait()
    w_t[...] = w_half[...].T
    loads[0].wait()
    for p in range(3):
        a, b, c = PARTS[p]
        received(block_of(tab, p, slice(0, 3), pos[b], pos[c]), ag_r.at[p, 15])

    def send_row_c(p, j, b_at):
        a, b, c = PARTS[p]
        row = row_of(tab, p, b_at, pos[c])
        for d, off in enumerate((1, -1)):
            send(row, row, ag_s.at[p], ag_r.at[p, 3 + 2 * j + d], peer(c, off))

    for p in range(3):
        a, b, c = PARTS[p]
        row = row_of(tab, p, pos[b], pos[c])
        for k, off in enumerate(OFFS):
            send(row, row, ag_s.at[p], ag_r.at[p, k], peer(b, off))
        send_row_c(p, 0, pos[b])

    def hidden_of(rows):
        hidden = lax.dot_general(w_t[...], vis[rows, :], NT, preferred_element_type=F32)
        value = jnp.tanh(hidden)
        squash[:, rows] = value
        coded[mine, rows] = value.astype(BF16)

    loads[2].wait()
    hidden_of(mine)

    for k, off in enumerate(OFFS):
        for p in range(3):
            a, b, c = PARTS[p]
            b_at = mod4(pos[b] - off)
            received(row_of(tab, p, b_at, pos[c]), ag_r.at[p, k])
            send_row_c(p, REL.index(-off if off != 2 else 2), b_at)

    received(vis.at[theirs], d2d_r.at[0])
    hidden_of(theirs)
    send(coded.at[mine], coded.at[mine], d2d_s.at[2], d2d_r.at[2], sibling)

    def take_row(j):
        for p in range(3):
            a, b, c = PARTS[p]
            b_at = mod4(pos[b] + REL[j])
            low = row_of(tab, p, b_at, mod4(pos[c] - 1))
            received(low, ag_r.at[p, 3 + 2 * j])
            if j in (0, 1):
                send(low, low, ag_s.at[p], ag_r.at[p, 11 + j], peer(c, 1))
            high = row_of(tab, p, b_at, mod4(pos[c] + 1))
            received(high, ag_r.at[p, 4 + 2 * j])
            if j in (2, 3):
                send(high, high, ag_s.at[p], ag_r.at[p, 11 + j], peer(c, -1))

    take_row(0)
    loads[4].wait()
    order_t[...] = own_order[...].astype(F32).T
    lane_q = lax.broadcasted_iota(jnp.int32, (32, 32), 1)
    lane_j = lax.broadcasted_iota(jnp.int32, (32, 128), 1)

    def select(n, _):
        bz, by, bx = n // 16, lax.rem(n // 4, 4), lax.rem(n, 4)
        q = (lax.rem(bx, 2) * 4 + by) * 4 + (bx // 2) * 2 + bz // 2
        m = lax.rem(bz, 2) * 2 + core
        rows = order_t[pl.ds(pl.multiple_of(m * 32, 32), 32), :]
        ids = jnp.sum(jnp.where(lane_q == q, rows, 0.0), axis=1, keepdims=True).astype(jnp.int32)
        ids = jnp.broadcast_to(ids, (32, 128))
        picked = jnp.where(lane_j == (ids >> 7), 1.0, 0.0)
        sel[n] = jnp.where(lane_j == 32, -(ids & 127).astype(F32), picked).astype(BF16)
        return 0

    lax.fori_loop(0, 64, select, 0)
    take_row(2)
    vis_t[...] = vis[...].T
    take_row(1)
    take_row(3)
    received(coded.at[theirs], d2d_r.at[2])
    received(lab.at[theirs], d2d_r.at[1])
    for j in (0, 1, 2, 3):
        for p in range(3):
            a, b, c = PARTS[p]
            row = row_of(tab, p, mod4(pos[b] + REL[j]), mod4(pos[c] + 2))
            received(row, ag_r.at[p, 11 + j])

    scale = 1.0 / 256.0

    def residual_of(plane, _):
        rows = tab[plane].reshape(512, 1024)
        picks = sel[pl.ds(plane * 16, 16)].reshape(512, 128)
        for half in range(2):
            seen = pl.ds(half * 512, 512)
            logits = lax.dot_general(rows, coded[:, seen], NN, preferred_element_type=F32)
            gap = lax.dot_general(picks, lab[seen, :], NT, preferred_element_type=F32)
            prob = 0.5 * jnp.tanh(0.5 * logits) + 0.5
            value = (prob - jnp.where(gap == 0.0, 1.0, 0.0)) * scale
            res[plane, :, :, :, seen] = value.astype(BF16).reshape(4, 4, 32, 512)
        tab_t[:, pl.ds(pl.multiple_of(plane * 512, 512), 512)] = rows.T
        return 0

    lax.fori_loop(0, 4, residual_of, 0)

    flat = res.reshape(2048, 1024)

    def coded_grad(at):
        rows = tab_t[pl.ds(pl.multiple_of(at, 128), 128), :]
        return lax.dot_general(rows, flat[...], NN, preferred_element_type=F32)

    def away(n, _):
        part = pl.ds(pl.multiple_of(n * 128, 128), 128)
        cg_out[part, :] = coded_grad((1 - core) * 512 + n * 128).astype(BF16)
        send(cg_out.at[part], cg_in.at[part], d2d_s.at[3], d2d_r.at[3], sibling)
        return 0

    lax.fori_loop(0, 4, away, 0)

    s, fp, own = (s0, s1, s2), (fp0, fp1, fp2), (own0, own1, own2)
    hb, rb = (hb0, hb1, hb2), (rb0, rb1, rb2)
    r2a, r2b, r2s, r3b = (r2a0, r2a1, r2a2), (r2b0, r2b1, r2b2), (r2s0, r2s1, r2s2), (r3b0, r3b1, r3b2)

    def term(p, off):
        c_at = mod4(pos[PARTS[p][2]] + off)
        rows = (res[c_at], res[:, :, c_at], res[:, c_at])[p].reshape(512, 1024)
        value = lax.dot_general(rows, coded[cols(p), :], NT, preferred_element_type=F32)
        return value.reshape(4, 4, 32, COLS[p][1])

    for p in range(3):
        a, b, c = PARTS[p]
        s[p][2] = term(p, 2).astype(BF16)
        for j in range(4):
            src = plane_row(s[p].at[2], p, mod4(pos[b] + REL[j]))
            send(src, hb[p].at[j], rs_s.at[p, 0], rs_r.at[p, j], peer(c, 1 if j < 2 else -1))

    def home(n, _):
        cg_own[pl.ds(pl.multiple_of(n * 128, 128), 128), :] = coded_grad(core * 512 + n * 128)
        return 0

    lax.fori_loop(0, 4, home, 0)
    received(cg_in, d2d_r.at[3])
    hgrad[...] = ((cg_own[...] + cg_in[...].astype(F32)) * (1.0 - squash[...] * squash[...])).astype(BF16)

    for half in range(2):
        value = lax.dot_general(vis_t[pl.ds(half * 512, 512), :], hgrad[...], NT, preferred_element_type=F32)
        wfull[:, pl.ds(half * 512, 512)] = value
        wlow[:, pl.ds(half * 512, 512)] = value.astype(BF16)
    w1b, wp, w2b, wq, w3b = (
        (w1b0, w1b1, w1b2), (wp0, wp1, wp2), (w2b0, w2b1, w2b2), (wq0, wq1, wq2), (w3b0, w3b1, w3b2)
    )

    def span(at, size):
        return pl.ds(pl.multiple_of(at * size, size), size)

    for k, off in enumerate(OFFS):
        for p in range(3):
            c = PARTS[p][2]
            src = wlow.at[span(mod4(pos[c] + off), 128), cols(p)]
            send(src, w1b[p].at[k], wt_s.at[p, 0], wt_r.at[p, 0], peer(c, off))

    def send_term_row(p, k, j):
        b, c = PARTS[p][1], PARTS[p][2]
        src = plane_row(s[p].at[k], p, mod4(pos[b] + REL[j]))
        send(src, rb[p].at[k, j], rs_s.at[p, 0], rs_r.at[p, 4 + 4 * k + j], peer(c, OFFS[k]))

    for k in range(2):
        for p in range(3):
            a, b, c = PARTS[p]
            value = term(p, OFFS[k])
            fp[p][k] = value
            s[p][k] = value.astype(BF16)
            for j in (2, 3) if k == 0 else (0, 1):
                send_term_row(p, k, j)

    for j in (0, 2, 1, 3):
        k = 0 if j < 2 else 1
        for p in range(3):
            a, b, c = PARTS[p]
            received(hb[p].at[j], rs_r.at[p, j])
            b_at = mod4(pos[b] + REL[j])
            whole = plane_row(fp[p].at[k], p, b_at)[...] + hb[p][j].astype(F32)
            plane_row(s[p].at[k], p, b_at)[...] = whole.astype(BF16)
            send_term_row(p, k, j)

    for p in range(3):
        c = PARTS[p][2]
        received(w1b[p], wt_r.at[p, 0])
        wp[p][...] = (
            wfull[span(pos[c], 128), cols(p)]
            + w1b[p][0].astype(F32) + w1b[p][1].astype(F32) + w1b[p][2].astype(F32)
        )
        b = PARTS[p][1]
        for k, off in enumerate(OFFS):
            src = wp[p].at[span(mod4(pos[b] + off), 32)]
            send(src, w2b[p].at[k], wt_s.at[p, 1], wt_r.at[p, 1], peer(b, off))

    for p in range(3):
        own[p][...] = term(p, 0)

    def sum_c(p):
        a, b, c = PARTS[p]
        for j in (2, 0, 1, 3):
            for k in range(2):
                received(rb[p].at[k, j], rs_r.at[p, 4 + 4 * k + j])
            mine_row = plane_row(own[p], p, mod4(pos[b] + REL[j]))
            mine_row[...] = mine_row[...] + rb[p][0, j].astype(F32) + rb[p][1, j].astype(F32)
        r2a[p][...] = own[p][...].astype(BF16)
        for k, off in enumerate(OFFS):
            src = plane_row(r2a[p], p, mod4(pos[b] + off))
            send(src, r2b[p].at[k], rs_s.at[p, 0], rs_r.at[p, 12], peer(b, off))

    for p in range(3):
        a, b, c = PARTS[p]
        received(w2b[p], wt_r.at[p, 1])
        wq[p][...] = wp[p][span(pos[b], 32), :] + w2b[p][0] + w2b[p][1] + w2b[p][2]
        for k, off in enumerate(OFFS):
            src = wq[p].at[span(mod4(pos[a] + off), 8)]
            send(src, w3b[p].at[k], wt_s.at[p, 1], wt_r.at[p, 2], peer(a, off))

    sum_c(0)

    for p in range(3):
        a, b, c = PARTS[p]
        received(w3b[p], wt_r.at[p, 2])
        at = span((pos[c] * 4 + pos[b]) * 4 + pos[a], 8)
        wout[at, cols(p)] = wq[p][span(pos[a], 8), :] + w3b[p][0] + w3b[p][1] + w3b[p][2]
        for k, off in enumerate(OFFS):
            block = wout.at[at, cols(p)]
            send(block, block, wt_s.at[p, 1], wt_r.at[p, 3], peer(a, off))

    sum_c(1)

    for p in range(3):
        a, b, c = PARTS[p]
        received(wout.at[pl.ds(0, 24), cols(p)], wt_r.at[p, 3])
        for k, off in enumerate(OFFS):
            row = wout.at[span(pos[c] * 4 + pos[b], 32), cols(p)]
            send(row, row, wt_s.at[p, 1], wt_r.at[p, 4], peer(b, off))

    sum_c(2)

    pieces = (((0, 0, 384),), ((384, 0, 128), (512, 1, 256)), ((768, 1, 256),))

    def deliver(p, c_at):
        for lo, half, size in pieces[p]:
            src = wout.at[span(c_at, 128), pl.ds(lo, size)]
            dst = wgrad.at[
                pl.ds(pl.multiple_of(half * 512 + c_at * 128, 128), 128),
                pl.ds(pl.multiple_of(core * 512 + lo - half * 512, 128), size),
            ]
            pltpu.make_async_copy(src, dst, out_sem.at[0]).start()
            send(src, dst, out_sem.at[1], out_sem.at[2], sibling)

    for p in range(3):
        a, b, c = PARTS[p]
        received(wout.at[pl.ds(0, 96), cols(p)], wt_r.at[p, 4])
        plane = wout.at[span(pos[c], 128), cols(p)]
        for k, off in enumerate((1, -1)):
            send(plane, plane, wt_s.at[p, 2], wt_r.at[p, 5 + k], peer(c, off))
        deliver(p, pos[c])

    for p in range(3):
        a, b, c = PARTS[p]
        received(r2b[p], rs_r.at[p, 12])
        r2s[p][...] = (
            plane_row(own[p], p, pos[b])[...] + r2b[p][0].astype(F32) + r2b[p][1].astype(F32) + r2b[p][2].astype(F32)
        )
        for k, off in enumerate(OFFS):
            send(r2s[p].at[mod4(pos[a] + off)], r3b[p].at[k], rs_s.at[p, 1], rs_r.at[p, 13], peer(a, off))

    for p in range(3):
        c = PARTS[p][2]
        for k, off in enumerate((1, -1)):
            at = mod4(pos[c] - off)
            received(wout.at[span(at, 128), cols(p)], wt_r.at[p, 5 + k])
            half = wout.at[span(at * 2 + k, 64), cols(p)]
            send(half, half, wt_s.at[p, 2], wt_r.at[p, 7 + k], peer(c, off))
            deliver(p, at)

    for p in range(3):
        a, b, c = PARTS[p]
        received(r3b[p], rs_r.at[p, 13])
        dgrad[:, cols(p)] = r2s[p][pos[a]] + r3b[p][0] + r3b[p][1] + r3b[p][2]

    for p in range(3):
        c = PARTS[p][2]
        at = mod4(pos[c] + 2)
        for k in range(2):
            received(wout.at[span(at * 2 + k, 64), cols(p)], wt_r.at[p, 7 + k])
        deliver(p, at)

    flat_tab = tab.reshape(64, 32, 1024)
    for p in range(3):
        received(flat_tab.at[pl.ds(0, 63), :, cols(p)], ag_s.at[p])
        received(flat_tab.at[pl.ds(0, 60), :, cols(p)], rs_s.at[p, 0])
        received(r3b[p], rs_s.at[p, 1])
        received(w1b[p], wt_s.at[p, 0])
        received(wout.at[pl.ds(0, 240), cols(p)], wt_s.at[p, 1])
        received(wout.at[pl.ds(0, 384), cols(p)], wt_s.at[p, 2])
    for n, ref in enumerate((vis.at[mine], lab.at[mine], coded.at[mine], cg_out)):
        received(ref, d2d_s.at[n])
    for n in range(3):
        received(wout, out_sem.at[n])


def per_part(make):
    return [make(width) for _, width in COLS]


def local(visits, enc_weight, drug_table, labels, drug_order):
    vmem = pltpu.VMEM
    scratch = [
        vmem((1024, 1024), BF16), vmem((1024, 1024), BF16), vmem((1024, 512), BF16), vmem((512, 1024), BF16),
        vmem((32, 128), jnp.int32), vmem((32, 512), jnp.int32), vmem((128, 32), F32),
        vmem((64, 32, 128), BF16), vmem((1024, 128), BF16), vmem((1024, 1024), BF16), vmem((512, 1024), F32),
        vmem((4, 4, 4, 32, 1024), BF16), vmem((1024, 2048), BF16), vmem((4, 4, 4, 32, 1024), BF16),
        vmem((512, 1024), BF16), vmem((512, 1024), BF16), vmem((512, 1024), F32), vmem((512, 1024), BF16),
        *per_part(lambda n: vmem((3, 4, 4, 32, n), BF16)),
        *per_part(lambda n: vmem((2, 4, 4, 32, n), F32)),
        *per_part(lambda n: vmem((4, 4, 32, n), F32)),
        *per_part(lambda n: vmem((4, 4, 32, n), BF16)),
        *per_part(lambda n: vmem((2, 4, 4, 32, n), BF16)),
        *per_part(lambda n: vmem((4, 4, 32, n), BF16)),
        *per_part(lambda n: vmem((3, 4, 32, n), BF16)),
        *per_part(lambda n: vmem((4, 32, n), F32)),
        *per_part(lambda n: vmem((3, 32, n), F32)),
        vmem((512, 1024), F32), vmem((512, 1024), BF16),
        *per_part(lambda n: vmem((3, 128, n), BF16)),
        *per_part(lambda n: vmem((128, n), F32)),
        *per_part(lambda n: vmem((3, 32, n), F32)),
        *per_part(lambda n: vmem((32, n), F32)),
        *per_part(lambda n: vmem((3, 8, n), F32)),
        vmem((512, 1024), F32),
        pltpu.SemaphoreType.DMA((5,)),
        pltpu.SemaphoreType.DMA((3,)), pltpu.SemaphoreType.DMA((3, 16)),
        pltpu.SemaphoreType.DMA((3, 2)), pltpu.SemaphoreType.DMA((3, 14)),
        pltpu.SemaphoreType.DMA((3, 3)), pltpu.SemaphoreType.DMA((3, 9)),
        pltpu.SemaphoreType.DMA((4,)), pltpu.SemaphoreType.DMA((4,)), pltpu.SemaphoreType.DMA((3,)),
    ]
    anywhere = pl.BlockSpec(memory_space=pl.ANY)
    return pl.pallas_call(
        kernel,
        name="step",
        out_shape=(jax.ShapeDtypeStruct((32, 1024), F32), jax.ShapeDtypeStruct((1024, 1024), F32)),
        in_specs=[anywhere] * 5,
        out_specs=(pl.BlockSpec(memory_space=pltpu.VMEM), anywhere),
        scratch_shapes=scratch,
        compiler_params=pltpu.CompilerParams(
            collective_id=0, has_side_effects=True, vmem_limit_bytes=60 * 2**20
        ),
    )(visits, enc_weight, drug_table, labels.T, drug_order.reshape(32, 128))


def solution(mesh):
    return jax.shard_map(
        local,
        mesh=mesh,
        in_specs=(
            P(("group", "inner"), None),
            P(),
            P(("group", "inner"), None),
            P(("group", "inner"), None),
            P(),
        ),
        out_specs=(P(("group", "inner"), None), P()),
        check_vma=False,
    )
```

```python
import math

import jax
import jax.numpy as jnp
from jax import lax
from jax.experimental import pallas as pl
from jax.experimental.pallas import tpu as pltpu
from jax.sharding import PartitionSpec as P

MESH = pl.DeviceIdType.MESH
F32 = jnp.float32
BF16 = jnp.bfloat16
NN = (((1,), (0,)), ((), ()))
NT = (((1,), (1,)), ((), ()))

PARTS = ((0, 1, 2), (1, 2, 0), (2, 0, 1))
COLS = ((0, 384), (384, 384), (768, 256))
OFFS = (1, -1, 2)
REL = (0, 1, -1, 2)
BACK = {1: 2, -1: 1, 2: 3}


def mod4(v):
    return lax.rem(v + 8, 4)


def kernel(
    visits, weight, table, labels, order, dgrad, wgrad,
    vis, vis_t, w_half, w_t, own_order, own_labels, order_t, sel, lab, coded, squash, tab, tab_t, res,
    cg_out, cg_in, cg_own, hgrad,
    s0, s1, s2, fp0, fp1, fp2, own0, own1, own2, hb0, hb1, hb2, rb0, rb1, rb2,
    r2a0, r2a1, r2a2, r2b0, r2b1, r2b2, r2s0, r2s1, r2s2,
    r3b0, r3b1, r3b2,
    wfull, wlow, w1b0, w1b1, w1b2, wp0, wp1, wp2, w2b0, w2b1, w2b2, w3b0, w3b1, w3b2, wout,
    load_sem, ag_s, ag_r, rs_s, rs_r, wt_s, wt_r, d2d_s, d2d_r, out_sem,
):
    g, i = lax.axis_index("group"), lax.axis_index("inner")
    x = (i // 8) * 2 + g // 4
    y = lax.rem(g, 4)
    z = lax.rem(i // 2, 4)
    core = lax.rem(i, 2)
    pos = (x, y, z)

    def device(px, py, pz, pc):
        return (lax.rem(px, 2) * 4 + py, (px // 2) * 8 + pz * 2 + pc)

    def peer_of(axis, off):
        moved = [mod4(v + off) if k == axis else v for k, v in enumerate(pos)]
        return device(*moved, core)

    peers = {(axis, off): peer_of(axis, off) for axis in range(3) for off in OFFS}

    def peer(axis, off):
        return peers[axis, off]

    places = {(axis, off): mod4(pos[axis] + off) if off else pos[axis] for axis in range(3) for off in REL}
    sibling = device(x, y, z, 1 - core)
    def send(src, dst, ssem, rsem, to):
        copy = pltpu.make_async_remote_copy(
            src_ref=src, dst_ref=dst, send_sem=ssem, recv_sem=rsem, device_id=to, device_id_type=MESH
        )
        copy.start()

    def received(dst, rsem):
        pltpu.make_async_copy(dst, dst, rsem).wait()

    def cols(p):
        return pl.ds(COLS[p][0], COLS[p][1])

    def row_of(buf, p, b_at, c_at, a_at=slice(None)):
        a, b, c = PARTS[p]
        at = [None, None, None]
        at[a], at[b], at[c] = a_at, b_at, c_at
        return buf.at[at[2], at[1], at[0], :, cols(p)]

    def plane_row(buf, p, b_at):
        return buf.at[:, b_at] if p == 2 else buf.at[b_at]

    mine = pl.ds(pl.multiple_of(core * 512, 512), 512)
    theirs = pl.ds(pl.multiple_of((1 - core) * 512, 512), 512)
    loads = [
        pltpu.make_async_copy(table, tab.at[0, 0, 0], load_sem.at[0]),
        pltpu.make_async_copy(weight.at[:, mine], w_half, load_sem.at[1]),
        pltpu.make_async_copy(visits, vis.at[mine], load_sem.at[2]),
        pltpu.make_async_copy(labels, own_labels, load_sem.at[3]),
        pltpu.make_async_copy(order, own_order, load_sem.at[4]),
    ]
    for load in loads:
        load.start()
    barrier = pltpu.get_barrier_semaphore()
    partners = [peer(axis, off) for axis in range(3) for off in OFFS] + [sibling]
    for partner in partners:
        pl.semaphore_signal(barrier, inc=1, device_id=partner, device_id_type=MESH)
    pl.semaphore_wait(barrier, len(partners))

    def own_block():
        for off in OFFS:
            for p in range(3):
                a, b, c = PARTS[p]
                send(table.at[:, cols(p)], row_of(tab, p, 0, 0, BACK[off]), ag_s.at[p], ag_r.at[p, 15], peer(a, off))

    def send_row_c(p, j):
        for d, off in enumerate((1, -1)):
            to = row_of(tab, p, j, BACK[off])
            send(row_of(tab, p, j, 0), to, ag_s.at[p], ag_r.at[p, 3 + 2 * j + d], peer(PARTS[p][2], off))

    def own_row():
        loads[0].wait()
        for p in range(3):
            received(row_of(tab, p, 0, 0, slice(1, 4)), ag_r.at[p, 15])
        for p in range(3):
            for k, off in enumerate(OFFS):
                to = row_of(tab, p, BACK[off], 0)
                send(row_of(tab, p, 0, 0), to, ag_s.at[p], ag_r.at[p, k], peer(PARTS[p][1], off))
            send_row_c(p, 0)

    def rows_of_b():
        for k, off in enumerate(OFFS):
            for p in range(3):
                received(row_of(tab, p, BACK[off], 0), ag_r.at[p, k])
                send_row_c(p, BACK[off])

    def rows_of_c(j):
        for p in range(3):
            for d, off in enumerate((1, -1)):
                row = row_of(tab, p, j, BACK[off])
                received(row, ag_r.at[p, 3 + 2 * j + d])
                if (j in (0, 1)) == (d == 0):
                    send(row, row_of(tab, p, j, 3), ag_s.at[p], ag_r.at[p, 11 + j], peer(PARTS[p][2], off))

    def far_rows():
        for j in range(4):
            for p in range(3):
                received(row_of(tab, p, j, 3), ag_r.at[p, 11 + j])

    def hidden_of(rows):
        hidden = lax.dot_general(w_t[...], vis[rows, :], NT, preferred_element_type=F32)
        value = jnp.tanh(hidden)
        squash[:, rows] = value
        coded[mine, rows] = value.astype(BF16)

    lane_q = lax.broadcasted_iota(jnp.int32, (32, 32), 1)
    lane_j = lax.broadcasted_iota(jnp.int32, (32, 128), 1)

    def away_by(v, at):
        return lax.rem(v + at + jnp.where(at == 2, 1, 0) - jnp.where(at == 3, 1, 0), 4)

    def select(n, _):
        bz, by, bx = away_by(z, n // 16), away_by(y, lax.rem(n // 4, 4)), away_by(x, lax.rem(n, 4))
        q = (lax.rem(bx, 2) * 4 + by) * 4 + (bx // 2) * 2 + bz // 2
        m = lax.rem(bz, 2) * 2 + core
        rows = order_t[pl.ds(pl.multiple_of(m * 32, 32), 32), :]
        ids = jnp.sum(jnp.where(lane_q == q, rows, 0.0), axis=1, keepdims=True).astype(jnp.int32)
        ids = jnp.broadcast_to(ids, (32, 128))
        picked = jnp.where(lane_j == (ids >> 7), 1.0, 0.0)
        sel[n // 16, lax.rem(n // 4, 4), lax.rem(n, 4)] = jnp.where(lane_j == 32, -(ids & 127).astype(F32), picked).astype(BF16)
        return 0

    scale = 1.0 / 256.0

    def residual_of(zs, ys, xs):
        shape = tuple(v.stop - v.start for v in (zs, ys, xs))
        count = shape[0] * shape[1] * shape[2] * 32
        rows = tab[zs, ys, xs].reshape(count, 1024)
        picks = sel[zs, ys, xs].reshape(count, 128)
        for half in range(2):
            seen = pl.ds(half * 512, 512)
            logits = lax.dot_general(rows, coded[:, seen], NN, preferred_element_type=F32)
            gap = lax.dot_general(picks, lab[seen, :], NT, preferred_element_type=F32)
            prob = 0.5 * jnp.tanh(0.5 * logits) + 0.5
            value = (prob - jnp.where(gap == 0.0, 1.0, 0.0)) * scale
            res[zs, ys, xs, :, seen] = value.astype(BF16).reshape(*shape, 32, 512)

    def turn(n, _):
        tab_t[:, pl.ds(pl.multiple_of(n * 512, 512), 512)] = tab[n].reshape(512, 1024).T
        return 0

    near, far, all_of = slice(0, 3), slice(3, 4), slice(0, 4)

    own_block()
    send(visits, vis.at[mine], d2d_s.at[0], d2d_r.at[0], sibling)
    loads[3].wait()
    column = lax.broadcasted_iota(jnp.int32, (32, 512), 0)
    ids_in_range = (own_labels[...] - column * 128).astype(F32)
    lab[mine, :] = jnp.concatenate([ids_in_range, jnp.ones((1, 512), F32), jnp.zeros((95, 512), F32)], axis=0).T.astype(BF16)
    send(lab.at[mine], lab.at[mine], d2d_s.at[1], d2d_r.at[1], sibling)
    own_row()
    loads[1].wait()
    w_t[...] = w_half[...].T
    loads[2].wait()
    hidden_of(mine)
    rows_of_b()
    received(vis.at[theirs], d2d_r.at[0])
    hidden_of(theirs)
    send(coded.at[mine], coded.at[mine], d2d_s.at[2], d2d_r.at[2], sibling)
    rows_of_c(0)
    loads[4].wait()
    order_t[...] = own_order[...].astype(F32).T
    lax.fori_loop(0, 64, select, 0)
    rows_of_c(2)
    vis_t[...] = vis[...].T
    rows_of_c(1)
    rows_of_c(3)
    received(coded.at[theirs], d2d_r.at[2])
    received(lab.at[theirs], d2d_r.at[1])

    for n in range(3):
        residual_of(slice(n, n + 1), near, near)
    far_rows()
    residual_of(far, all_of, all_of)
    residual_of(near, far, all_of)
    residual_of(near, near, far)
    lax.fori_loop(0, 4, turn, 0)

    flat = res.reshape(2048, 1024)

    def coded_grad(at):
        rows = tab_t[pl.ds(pl.multiple_of(at, 128), 128), :]
        return lax.dot_general(rows, flat[...], NN, preferred_element_type=F32)

    def away(n, _):
        part = pl.ds(pl.multiple_of(n * 128, 128), 128)
        cg_out[part, :] = coded_grad((1 - core) * 512 + n * 128).astype(BF16)
        send(cg_out.at[part], cg_in.at[part], d2d_s.at[3], d2d_r.at[3], sibling)
        return 0

    lax.fori_loop(0, 4, away, 0)

    s, fp, own = (s0, s1, s2), (fp0, fp1, fp2), (own0, own1, own2)
    hb, rb = (hb0, hb1, hb2), (rb0, rb1, rb2)
    r2a, r2b, r2s, r3b = (r2a0, r2a1, r2a2), (r2b0, r2b1, r2b2), (r2s0, r2s1, r2s2), (r3b0, r3b1, r3b2)

    def term(p, at):
        rows = (res[at], res[:, :, at], res[:, at])[p].reshape(512, 1024)
        value = lax.dot_general(rows, coded[cols(p), :], NT, preferred_element_type=F32)
        return value.reshape(4, 4, 32, COLS[p][1])

    for p in range(3):
        s[p][2] = term(p, 3).astype(BF16)
        for j in range(4):
            src = plane_row(s[p].at[2], p, j)
            send(src, hb[p].at[j], rs_s.at[p, 0], rs_r.at[p, j], peer(PARTS[p][2], 1 if j < 2 else -1))

    def home(n, _):
        cg_own[pl.ds(pl.multiple_of(n * 128, 128), 128), :] = coded_grad(core * 512 + n * 128)
        return 0

    lax.fori_loop(0, 4, home, 0)
    received(cg_in, d2d_r.at[3])
    hgrad[...] = ((cg_own[...] + cg_in[...].astype(F32)) * (1.0 - squash[...] * squash[...])).astype(BF16)

    for half in range(2):
        value = lax.dot_general(vis_t[pl.ds(half * 512, 512), :], hgrad[...], NT, preferred_element_type=F32)
        wfull[:, pl.ds(half * 512, 512)] = value
        wlow[:, pl.ds(half * 512, 512)] = value.astype(BF16)
    w1b, wp, w2b, w3b = (w1b0, w1b1, w1b2), (wp0, wp1, wp2), (w2b0, w2b1, w2b2), (w3b0, w3b1, w3b2)

    def span(at, size):
        return pl.ds(pl.multiple_of(at * size, size), size)

    def w_row(c_at, b_at):
        return span(c_at * 4 + b_at, 32)

    for j in (1, 2, 3, 0):
        for k, off in enumerate(OFFS):
            for p in range(3):
                a, b, c = PARTS[p]
                src = wlow.at[w_row(places[c, off], places[b, REL[j]]), cols(p)]
                send(src, w1b[p].at[j, k], wt_s.at[p, 0], wt_r.at[p, j], peer(c, off))

    def w_sum_c():
        for j in (1, 2, 3, 0):
            for p in range(3):
                a, b, c = PARTS[p]
                received(w1b[p].at[j], wt_r.at[p, j])
                wp[p][j] = (
                    wfull[w_row(pos[c], places[b, REL[j]]), cols(p)]
                    + w1b[p][j, 0].astype(F32) + w1b[p][j, 1].astype(F32) + w1b[p][j, 2].astype(F32)
                )
                if j:
                    send(wp[p].at[j], w2b[p].at[j - 1], wt_s.at[p, 1], wt_r.at[p, 4], peer(b, REL[j]))

    def w_sum_b():
        for p in range(3):
            a, b, c = PARTS[p]
            received(w2b[p], wt_r.at[p, 4])
            w3b[p][pos[a]] = wp[p][0] + w2b[p][0] + w2b[p][1] + w2b[p][2]
            own_slot = w3b[p].at[pos[a]]
            for off in OFFS:
                send(own_slot, own_slot, wt_s.at[p, 1], wt_r.at[p, 5], peer(a, off))

    def w_send_c(p, j):
        a, b, c = PARTS[p]
        row = wout.at[w_row(0, places[b, REL[j]]), cols(p)]
        for d, off in enumerate((1, -1)):
            send(row, wout.at[w_row(BACK[off], places[b, REL[j]]), cols(p)], wt_s.at[p, 2], wt_r.at[p, 9 + 2 * j + d], peer(c, off))

    def w_sum_a():
        for p in range(3):
            a, b, c = PARTS[p]
            received(w3b[p].at[pl.ds(0, 3)], wt_r.at[p, 5])
            at = w_row(0, pos[b])
            wout[at, cols(p)] = w3b[p][0] + w3b[p][1] + w3b[p][2] + w3b[p][3]
            row = wout.at[at, cols(p)]
            for k, off in enumerate(OFFS):
                send(row, row, wt_s.at[p, 2], wt_r.at[p, 6 + k], peer(b, off))
            w_send_c(p, 0)

    pieces = (((0, 0, 384),), ((384, 0, 128), (512, 1, 256)), ((768, 1, 256),))

    def deliver(p, at):
        c_at = places[PARTS[p][2], REL[at]]
        for lo, half, size in pieces[p]:
            src = wout.at[pl.ds(at * 128, 128), pl.ds(lo, size)]
            dst = wgrad.at[
                pl.ds(pl.multiple_of(half * 512 + c_at * 128, 128), 128),
                pl.ds(pl.multiple_of(core * 512 + lo - half * 512, 128), size),
            ]
            pltpu.make_async_copy(src, dst, out_sem.at[0]).start()
            send(src, dst, out_sem.at[1], out_sem.at[2], sibling)

    def w_take_b():
        for k, off in enumerate(OFFS):
            for p in range(3):
                j = BACK[off]
                received(wout.at[w_row(0, places[PARTS[p][1], REL[j]]), cols(p)], wt_r.at[p, 6 + k])
                w_send_c(p, j)
        for p in range(3):
            deliver(p, 0)

    def w_take_c():
        for j in (0, 2, 1, 3):
            for p in range(3):
                a, b, c = PARTS[p]
                for d, off in enumerate((1, -1)):
                    row = wout.at[w_row(BACK[off], places[b, REL[j]]), cols(p)]
                    received(row, wt_r.at[p, 9 + 2 * j + d])
                    if (j in (0, 1)) == (d == 0):
                        to = wout.at[w_row(3, places[b, REL[j]]), cols(p)]
                        send(row, to, wt_s.at[p, 2], wt_r.at[p, 17 + j], peer(c, off))
        for p in range(3):
            deliver(p, 1)
            deliver(p, 2)

    def w_take_far():
        for p in range(3):
            for j in range(4):
                received(wout.at[w_row(3, places[PARTS[p][1], REL[j]]), cols(p)], wt_r.at[p, 17 + j])
            deliver(p, 3)

    def send_term_row(p, k, j):
        src = plane_row(s[p].at[k], p, j)
        send(src, rb[p].at[k, j], rs_s.at[p, 0], rs_r.at[p, 4 + 4 * k + j], peer(PARTS[p][2], OFFS[k]))

    def near_terms(k):
        for p in range(3):
            value = term(p, 1 + k)
            fp[p][k] = value
            s[p][k] = value.astype(BF16)
            for j in (2, 3) if k == 0 else (0, 1):
                send_term_row(p, k, j)

    def pass_on(j):
        k = 0 if j < 2 else 1
        for p in range(3):
            received(hb[p].at[j], rs_r.at[p, j])
            whole = plane_row(fp[p].at[k], p, j)[...] + hb[p][j].astype(F32)
            plane_row(s[p].at[k], p, j)[...] = whole.astype(BF16)
            send_term_row(p, k, j)

    def own_terms():
        for p in range(3):
            own[p][...] = term(p, 0)

    def sum_c(p):
        a, b, c = PARTS[p]
        for j in (2, 0, 1, 3):
            for k in range(2):
                received(rb[p].at[k, j], rs_r.at[p, 4 + 4 * k + j])
            mine_row = plane_row(own[p], p, j)
            mine_row[...] = mine_row[...] + rb[p][0, j].astype(F32) + rb[p][1, j].astype(F32)
        r2a[p][...] = own[p][...].astype(BF16)
        for k, off in enumerate(OFFS):
            src = plane_row(r2a[p], p, REL.index(off))
            send(src, r2b[p].at[k], rs_s.at[p, 0], rs_r.at[p, 12], peer(b, off))

    def sum_b():
        for p in range(3):
            a, b, c = PARTS[p]
            received(r2b[p], rs_r.at[p, 12])
            r2s[p][...] = (
                plane_row(own[p], p, 0)[...]
                + r2b[p][0].astype(F32) + r2b[p][1].astype(F32) + r2b[p][2].astype(F32)
            )
            for k, off in enumerate(OFFS):
                send(r2s[p].at[REL.index(off)], r3b[p].at[k], rs_s.at[p, 1], rs_r.at[p, 13], peer(a, off))

    def sum_a():
        for p in range(3):
            a, b, c = PARTS[p]
            received(r3b[p], rs_r.at[p, 13])
            dgrad[:, cols(p)] = r2s[p][0] + r3b[p][0] + r3b[p][1] + r3b[p][2]

    near_terms(0)
    near_terms(1)
    w_sum_c()
    own_terms()
    pass_on(0)
    pass_on(2)
    w_sum_b()
    pass_on(1)
    pass_on(3)
    w_sum_a()
    sum_c(0)
    w_take_b()
    sum_c(1)
    sum_c(2)
    w_take_c()
    sum_b()
    w_take_far()
    sum_a()

    flat_tab = tab.reshape(64, 32, 1024)
    for p in range(3):
        received(flat_tab.at[pl.ds(0, 63), :, cols(p)], ag_s.at[p])
        received(flat_tab.at[pl.ds(0, 60), :, cols(p)], rs_s.at[p, 0])
        received(r3b[p], rs_s.at[p, 1])
        received(w1b[p], wt_s.at[p, 0])
        received(wout.at[pl.ds(0, 192), cols(p)], wt_s.at[p, 1])
        received(wout.at[pl.ds(0, 480), cols(p)], wt_s.at[p, 2])
    for n, ref in enumerate((vis.at[mine], lab.at[mine], coded.at[mine], cg_out)):
        received(ref, d2d_s.at[n])
    for n in range(3):
        received(wout, out_sem.at[n])


def per_part(make):
    return [make(width) for _, width in COLS]


def local(visits, enc_weight, drug_table, labels, drug_order):
    vmem = pltpu.VMEM
    scratch = [
        vmem((1024, 1024), BF16), vmem((1024, 1024), BF16), vmem((1024, 512), BF16), vmem((512, 1024), BF16),
        vmem((32, 128), jnp.int32), vmem((32, 512), jnp.int32), vmem((128, 32), F32),
        vmem((4, 4, 4, 32, 128), BF16), vmem((1024, 128), BF16), vmem((1024, 1024), BF16), vmem((512, 1024), F32),
        vmem((4, 4, 4, 32, 1024), BF16), vmem((1024, 2048), BF16), vmem((4, 4, 4, 32, 1024), BF16),
        vmem((512, 1024), BF16), vmem((512, 1024), BF16), vmem((512, 1024), F32), vmem((512, 1024), BF16),
        *per_part(lambda n: vmem((3, 4, 4, 32, n), BF16)),
        *per_part(lambda n: vmem((2, 4, 4, 32, n), F32)),
        *per_part(lambda n: vmem((4, 4, 32, n), F32)),
        *per_part(lambda n: vmem((4, 4, 32, n), BF16)),
        *per_part(lambda n: vmem((2, 4, 4, 32, n), BF16)),
        *per_part(lambda n: vmem((4, 4, 32, n), BF16)),
        *per_part(lambda n: vmem((3, 4, 32, n), BF16)),
        *per_part(lambda n: vmem((4, 32, n), F32)),
        *per_part(lambda n: vmem((3, 32, n), F32)),
        vmem((512, 1024), F32), vmem((512, 1024), BF16),
        *per_part(lambda n: vmem((4, 3, 32, n), BF16)),
        *per_part(lambda n: vmem((4, 32, n), F32)),
        *per_part(lambda n: vmem((3, 32, n), F32)),
        *per_part(lambda n: vmem((4, 32, n), F32)),
        vmem((512, 1024), F32),
        pltpu.SemaphoreType.DMA((5,)),
        pltpu.SemaphoreType.DMA((3,)), pltpu.SemaphoreType.DMA((3, 16)),
        pltpu.SemaphoreType.DMA((3, 2)), pltpu.SemaphoreType.DMA((3, 14)),
        pltpu.SemaphoreType.DMA((3, 3)), pltpu.SemaphoreType.DMA((3, 21)),
        pltpu.SemaphoreType.DMA((4,)), pltpu.SemaphoreType.DMA((4,)), pltpu.SemaphoreType.DMA((3,)),
    ]
    anywhere = pl.BlockSpec(memory_space=pl.ANY)
    return pl.pallas_call(
        kernel,
        name="step",
        out_shape=(pltpu.VMEM((32, 1024), F32), pltpu.VMEM((1024, 1024), F32)),
        in_specs=[anywhere] * 5,
        out_specs=[pl.BlockSpec(memory_space=pltpu.VMEM)] * 2,
        scratch_shapes=scratch,
        compiler_params=pltpu.CompilerParams(
            collective_id=0, has_side_effects=True, vmem_limit_bytes=54 * 2**20
        ),
    )(visits, enc_weight, drug_table, labels.T, drug_order.reshape(32, 128))


def solution(mesh):
    return jax.shard_map(
        local,
        mesh=mesh,
        in_specs=(
            P(("group", "inner"), None),
            P(),
            P(("group", "inner"), None),
            P(("group", "inner"), None),
            P(),
        ),
        out_specs=(P(("group", "inner"), None), P()),
        check_vma=False,
    )
```

```python
import math

import jax
import jax.numpy as jnp
from jax import lax
from jax.experimental import pallas as pl
from jax.experimental.pallas import tpu as pltpu
from jax.sharding import PartitionSpec as P

MESH = pl.DeviceIdType.MESH
F32 = jnp.float32
BF16 = jnp.bfloat16
NN = (((1,), (0,)), ((), ()))
NT = (((1,), (1,)), ((), ()))

PARTS = ((0, 1, 2), (1, 2, 0), (2, 0, 1))
COLS = ((0, 384), (384, 384), (768, 256))
OFFS = (1, -1, 2)
REL = (0, 1, -1, 2)
BACK = {1: 2, -1: 1, 2: 3}


STEPS = 780.0
FLOOR = 20.0


def encode(value):
    size = jnp.maximum(jnp.abs(value), 2.0**-FLOOR)
    code = jnp.minimum(jnp.round((jnp.log2(size) + FLOOR) * STEPS), 32767.0)
    return jnp.where(value < 0.0, -code, code).astype(jnp.int32).astype(jnp.int16)


def decode(code):
    code = code.astype(jnp.int32).astype(F32)
    size = jnp.exp2(jnp.abs(code) * (1.0 / STEPS) - FLOOR)
    return jnp.where(code == 0.0, 0.0, jnp.where(code < 0.0, -size, size))


def mod4(v):
    return lax.rem(v + 8, 4)


def kernel(
    visits, weight, table, labels, order, dgrad, wgrad,
    vis, vis_t, w_half, w_t, own_order, own_labels, order_t, sel, lab, coded, squash, tab, tab_t, res,
    cg_out, cg_in, cg_own, hgrad,
    s0, s1, s2, fp0, fp1, fp2, own0, own1, own2, hb0, hb1, hb2, rb0, rb1, rb2,
    r2a0, r2a1, r2a2, r2b0, r2b1, r2b2, r2s0, r2s1, r2s2,
    r3b0, r3b1, r3b2,
    wfull, wlow, w1b0, w1b1, w1b2, wp0, wp1, wp2, wc0, wc1, wc2, w2b0, w2b1, w2b2, w3b0, w3b1, w3b2, wout, wsib,
    load_sem, ag_s, ag_r, rs_s, rs_r, wt_s, wt_r, d2d_s, d2d_r, out_s, out_r,
):
    g, i = lax.axis_index("group"), lax.axis_index("inner")
    x = (i // 8) * 2 + g // 4
    y = lax.rem(g, 4)
    z = lax.rem(i // 2, 4)
    core = lax.rem(i, 2)
    pos = (x, y, z)

    def device(px, py, pz, pc):
        return (lax.rem(px, 2) * 4 + py, (px // 2) * 8 + pz * 2 + pc)

    def peer_of(axis, off):
        moved = [mod4(v + off) if k == axis else v for k, v in enumerate(pos)]
        return device(*moved, core)

    peers = {(axis, off): peer_of(axis, off) for axis in range(3) for off in OFFS}

    def peer(axis, off):
        return peers[axis, off]

    places = {(axis, off): mod4(pos[axis] + off) if off else pos[axis] for axis in range(3) for off in REL}
    sibling = device(x, y, z, 1 - core)
    def send(src, dst, ssem, rsem, to):
        copy = pltpu.make_async_remote_copy(
            src_ref=src, dst_ref=dst, send_sem=ssem, recv_sem=rsem, device_id=to, device_id_type=MESH
        )
        copy.start()

    def received(dst, rsem):
        pltpu.make_async_copy(dst, dst, rsem).wait()

    def cols(p):
        return pl.ds(COLS[p][0], COLS[p][1])

    def row_of(buf, p, b_at, c_at, a_at=slice(None)):
        a, b, c = PARTS[p]
        at = [None, None, None]
        at[a], at[b], at[c] = a_at, b_at, c_at
        return buf.at[at[2], at[1], at[0], :, cols(p)]

    def plane_row(buf, p, b_at):
        return buf.at[:, b_at] if p == 2 else buf.at[b_at]

    mine = pl.ds(pl.multiple_of(core * 512, 512), 512)
    theirs = pl.ds(pl.multiple_of((1 - core) * 512, 512), 512)
    loads = [
        pltpu.make_async_copy(table, tab.at[0, 0, 0], load_sem.at[0]),
        pltpu.make_async_copy(weight.at[:, mine], w_half, load_sem.at[1]),
        pltpu.make_async_copy(visits, vis.at[mine], load_sem.at[2]),
        pltpu.make_async_copy(labels, own_labels, load_sem.at[3]),
        pltpu.make_async_copy(order, own_order, load_sem.at[4]),
    ]
    for load in loads:
        load.start()
    barrier = pltpu.get_barrier_semaphore()
    partners = [peer(axis, off) for axis in range(3) for off in OFFS] + [sibling]
    for partner in partners:
        pl.semaphore_signal(barrier, inc=1, device_id=partner, device_id_type=MESH)
    pl.semaphore_wait(barrier, len(partners))

    def own_block():
        for p in range(3):
            a, b, c = PARTS[p]
            block = table.at[:, cols(p)]
            for off in OFFS:
                send(block, row_of(tab, p, 0, 0, BACK[off]), ag_s.at[p], ag_r.at[p, 12], peer(a, off))
        for p in range(3):
            a, b, c = PARTS[p]
            block = table.at[:, cols(p)]
            for k, off in enumerate(OFFS):
                send(block, row_of(tab, p, BACK[off], 0, 0), ag_s.at[p], ag_r.at[p, k], peer(b, off))
            for d, off in enumerate((1, -1)):
                send(block, row_of(tab, p, 0, BACK[off], 0), ag_s.at[p], ag_r.at[p, 3 + d], peer(c, off))

    def send_row_c(p, j):
        part = slice(None) if j else slice(1, 4)
        for d, off in enumerate((1, -1)):
            to = row_of(tab, p, j, BACK[off], part)
            send(row_of(tab, p, j, 0, part), to, ag_s.at[p], ag_r.at[p, 3 + 2 * j + d], peer(PARTS[p][2], off))

    def own_row():
        loads[0].wait()
        rest = slice(1, 4)
        for p in range(3):
            received(row_of(tab, p, 0, 0, rest), ag_r.at[p, 12])
        for p in range(3):
            for k, off in enumerate(OFFS):
                to = row_of(tab, p, BACK[off], 0, rest)
                send(row_of(tab, p, 0, 0, rest), to, ag_s.at[p], ag_r.at[p, k], peer(PARTS[p][1], off))
            send_row_c(p, 0)

    def rows_of_b():
        for k, off in enumerate(OFFS):
            for p in range(3):
                received(row_of(tab, p, BACK[off], 0), ag_r.at[p, k])
                send_row_c(p, BACK[off])

    def rows_of_c(j):
        for p in range(3):
            for d, off in enumerate((1, -1)):
                row = row_of(tab, p, j, BACK[off])
                received(row, ag_r.at[p, 3 + 2 * j + d])
                if (j in (0, 1)) == (d == 0):
                    send(row, row_of(tab, p, j, 3), ag_s.at[p], ag_r.at[p, 11], peer(PARTS[p][2], off))

    def far_rows():
        for p in range(3):
            received(row_of(tab, p, slice(None), 3), ag_r.at[p, 11])

    def hidden_of(rows):
        hidden = lax.dot_general(w_t[...], vis[rows, :], NT, preferred_element_type=F32)
        value = jnp.tanh(hidden)
        squash[:, rows] = value
        coded[mine, rows] = value.astype(BF16)

    lane_q = lax.broadcasted_iota(jnp.int32, (32, 32), 1)
    lane_j = lax.broadcasted_iota(jnp.int32, (32, 128), 1)

    def away_by(v, at):
        return lax.rem(v + at + jnp.where(at == 2, 1, 0) - jnp.where(at == 3, 1, 0), 4)

    def select(n, _):
        bz, by, bx = away_by(z, n // 16), away_by(y, lax.rem(n // 4, 4)), away_by(x, lax.rem(n, 4))
        q = (lax.rem(bx, 2) * 4 + by) * 4 + (bx // 2) * 2 + bz // 2
        m = lax.rem(bz, 2) * 2 + core
        rows = order_t[pl.ds(pl.multiple_of(m * 32, 32), 32), :]
        ids = jnp.sum(jnp.where(lane_q == q, rows, 0.0), axis=1, keepdims=True).astype(jnp.int32)
        ids = jnp.broadcast_to(ids, (32, 128))
        picked = jnp.where(lane_j == (ids >> 7), 1.0, 0.0)
        sel[n // 16, lax.rem(n // 4, 4), lax.rem(n, 4)] = jnp.where(lane_j == 32, -(ids & 127).astype(F32), picked).astype(BF16)
        return 0

    scale = 1.0 / 256.0

    def residual_of(zs, ys, xs):
        shape = tuple(v.stop - v.start for v in (zs, ys, xs))
        count = shape[0] * shape[1] * shape[2] * 32
        rows = tab[zs, ys, xs].reshape(count, 1024)
        picks = sel[zs, ys, xs].reshape(count, 128)
        for half in range(2):
            seen = pl.ds(half * 512, 512)
            logits = lax.dot_general(rows, coded[:, seen], NN, preferred_element_type=F32)
            gap = lax.dot_general(picks, lab[seen, :], NT, preferred_element_type=F32)
            prob = 0.5 * jnp.tanh(0.5 * logits) + 0.5
            value = (prob - jnp.where(gap == 0.0, 1.0, 0.0)) * scale
            res[zs, ys, xs, :, seen] = value.astype(BF16).reshape(*shape, 32, 512)

    def turn(n):
        tab_t[:, pl.ds(n * 512, 512)] = tab[n].reshape(512, 1024).T

    near, far, all_of = slice(0, 3), slice(3, 4), slice(0, 4)

    own_block()
    send(visits, vis.at[mine], d2d_s.at[0], d2d_r.at[0], sibling)
    loads[3].wait()
    column = lax.broadcasted_iota(jnp.int32, (32, 512), 0)
    ids_in_range = (own_labels[...] - column * 128).astype(F32)
    lab[mine, :] = jnp.concatenate([ids_in_range, jnp.ones((1, 512), F32), jnp.zeros((95, 512), F32)], axis=0).T.astype(BF16)
    send(lab.at[mine], lab.at[mine], d2d_s.at[1], d2d_r.at[1], sibling)
    own_row()
    loads[1].wait()
    w_t[...] = w_half[...].T
    loads[2].wait()
    hidden_of(mine)
    rows_of_b()
    received(vis.at[theirs], d2d_r.at[0])
    hidden_of(theirs)
    send(coded.at[mine], coded.at[mine], d2d_s.at[2], d2d_r.at[2], sibling)
    rows_of_c(0)
    loads[4].wait()
    order_t[...] = own_order[...].astype(F32).T
    lax.fori_loop(0, 64, select, 0)
    rows_of_c(2)
    vis_t[...] = vis[...].T
    rows_of_c(1)
    rows_of_c(3)
    received(coded.at[theirs], d2d_r.at[2])
    received(lab.at[theirs], d2d_r.at[1])

    for n in range(3):
        residual_of(slice(n, n + 1), near, near)
    far_rows()
    turn(3)
    residual_of(far, all_of, all_of)
    turn(0)
    turn(1)
    residual_of(near, far, all_of)
    turn(2)
    residual_of(near, near, far)

    flat = res.reshape(2048, 1024)

    def coded_grad(rows, seen):
        return lax.dot_general(tab_t[rows, :], flat[:, seen], NN, preferred_element_type=F32)

    def away():
        for n in range(2):
            seen = pl.ds(n * 512, 512)
            cg_out[:, seen] = coded_grad(theirs, seen).astype(BF16)
            send(cg_out.at[:, seen], cg_in.at[:, seen], d2d_s.at[3], d2d_r.at[3], sibling)

    s, fp, own = (s0, s1, s2), (fp0, fp1, fp2), (own0, own1, own2)
    hb, rb = (hb0, hb1, hb2), (rb0, rb1, rb2)
    r2a, r2b, r2s, r3b = (r2a0, r2a1, r2a2), (r2b0, r2b1, r2b2), (r2s0, r2s1, r2s2), (r3b0, r3b1, r3b2)

    def term(p, at):
        rows = (res[at], res[:, :, at], res[:, at])[p].reshape(512, 1024)
        value = lax.dot_general(rows, coded[cols(p), :], NT, preferred_element_type=F32)
        return value.reshape(4, 4, 32, COLS[p][1])

    def far_terms():
        for p in range(3):
            s[p][2] = term(p, 3).astype(BF16)
            for j in range(4):
                src = plane_row(s[p].at[2], p, j)
                send(src, hb[p].at[j], rs_s.at[p, 0], rs_r.at[p, j], peer(PARTS[p][2], 1 if j < 2 else -1))

    def weight_terms():
        cg_own[...] = coded_grad(mine, slice(None))
        received(cg_in, d2d_r.at[3])
        hgrad[...] = ((cg_own[...] + cg_in[...].astype(F32)) * (1.0 - squash[...] * squash[...])).astype(BF16)
        for half in range(2):
            value = lax.dot_general(vis_t[pl.ds(half * 512, 512), :], hgrad[...], NT, preferred_element_type=F32)
            wfull[:, pl.ds(half * 512, 512)] = value
            wlow[:, pl.ds(half * 512, 512)] = value.astype(BF16)

    w1b, wp, wc = (w1b0, w1b1, w1b2), (wp0, wp1, wp2), (wc0, wc1, wc2)
    w2b, w3b = (w2b0, w2b1, w2b2), (w3b0, w3b1, w3b2)

    def span(at, size):
        return pl.ds(pl.multiple_of(at * size, size), size)

    def w_row(c_at, b_at):
        return span(c_at * 4 + b_at, 32)

    def w_send_rows():
      for j in (1, 2, 3, 0):
        for k, off in enumerate(OFFS):
            for p in range(3):
                a, b, c = PARTS[p]
                src = wlow.at[w_row(places[c, off], places[b, REL[j]]), cols(p)]
                send(src, w1b[p].at[j, k], wt_s.at[p, 0], wt_r.at[p, j], peer(c, off))

    def w_sum_c():
        for j in (1, 2, 3, 0):
            for p in range(3):
                a, b, c = PARTS[p]
                received(w1b[p].at[j], wt_r.at[p, j])
                whole = (
                    wfull[w_row(pos[c], places[b, REL[j]]), cols(p)]
                    + w1b[p][j, 0].astype(F32) + w1b[p][j, 1].astype(F32) + w1b[p][j, 2].astype(F32)
                )
                if j:
                    wc[p][j - 1] = encode(whole)
                    send(wc[p].at[j - 1], w2b[p].at[j - 1], wt_s.at[p, 1], wt_r.at[p, 4], peer(b, REL[j]))
                else:
                    wp[p][...] = whole

    def w_sum_b():
        for p in range(3):
            a, b, c = PARTS[p]
            received(w2b[p], wt_r.at[p, 4])
            w3b[p][pos[a]] = encode(wp[p][...] + decode(w2b[p][0]) + decode(w2b[p][1]) + decode(w2b[p][2]))
            own_slot = w3b[p].at[pos[a]]
            for off in OFFS:
                send(own_slot, own_slot, wt_s.at[p, 1], wt_r.at[p, 5], peer(a, off))

    def w_send_c(p, j):
        a, b, c = PARTS[p]
        row = wout.at[w_row(0, places[b, REL[j]]), cols(p)]
        for d, off in enumerate((1, -1)):
            send(row, wout.at[w_row(BACK[off], places[b, REL[j]]), cols(p)], wt_s.at[p, 2], wt_r.at[p, 9 + 2 * j + d], peer(c, off))

    def w_sum_a():
        for p in range(3):
            a, b, c = PARTS[p]
            received(w3b[p].at[pl.ds(0, 3)], wt_r.at[p, 5])
            at = w_row(0, pos[b])
            wout[at, cols(p)] = encode(decode(w3b[p][0]) + decode(w3b[p][1]) + decode(w3b[p][2]) + decode(w3b[p][3]))
            row = wout.at[at, cols(p)]
            for k, off in enumerate(OFFS):
                send(row, row, wt_s.at[p, 2], wt_r.at[p, 6 + k], peer(b, off))
            w_send_c(p, 0)

    pieces = (((0, 0, 384),), ((384, 0, 128), (512, 1, 256)), ((768, 1, 256),))

    def deliver(p, at):
        src = wout.at[pl.ds(at * 128, 128), cols(p)]
        send(src, wsib.at[pl.ds(at * 128, 128), cols(p)], out_s.at[0], out_r.at[p, at], sibling)

    def put(buf, column, p, at):
        c_at = places[PARTS[p][2], REL[at]]
        for lo, half, size in pieces[p]:
            rows = pl.ds(pl.multiple_of(half * 512 + c_at * 128, 128), 128)
            lanes = pl.ds(pl.multiple_of(column * 512 + lo - half * 512, 128), size)
            wgrad[rows, lanes] = decode(buf[pl.ds(at * 128, 128), pl.ds(lo, size)])

    def put_own(at):
        for p in range(3):
            put(wout, core, p, at)

    def put_sibling(at):
        for p in range(3):
            received(wsib.at[pl.ds(at * 128, 128), cols(p)], out_r.at[p, at])
            put(wsib, 1 - core, p, at)

    def w_take_b():
        for k, off in enumerate(OFFS):
            for p in range(3):
                j = BACK[off]
                received(wout.at[w_row(0, places[PARTS[p][1], REL[j]]), cols(p)], wt_r.at[p, 6 + k])
                w_send_c(p, j)
        for p in range(3):
            deliver(p, 0)

    def w_take_c():
        for j in (0, 2, 1, 3):
            for p in range(3):
                a, b, c = PARTS[p]
                for d, off in enumerate((1, -1)):
                    row = wout.at[w_row(BACK[off], places[b, REL[j]]), cols(p)]
                    received(row, wt_r.at[p, 9 + 2 * j + d])
                    if (j in (0, 1)) == (d == 0):
                        to = wout.at[w_row(3, places[b, REL[j]]), cols(p)]
                        send(row, to, wt_s.at[p, 2], wt_r.at[p, 17], peer(c, off))
        for p in range(3):
            deliver(p, 1)
            deliver(p, 2)

    def w_take_far():
        for p in range(3):
            received(wout.at[pl.ds(384, 128), cols(p)], wt_r.at[p, 17])
            deliver(p, 3)

    def send_term_row(p, k, j):
        src = plane_row(s[p].at[k], p, j)
        send(src, rb[p].at[k, j], rs_s.at[p, 0], rs_r.at[p, 4], peer(PARTS[p][2], OFFS[k]))

    def near_terms(k):
        for p in range(3):
            value = term(p, 1 + k)
            fp[p][k] = value
            s[p][k] = value.astype(BF16)
            for j in (2, 3) if k == 0 else (0, 1):
                send_term_row(p, k, j)

    def pass_on(j):
        k = 0 if j < 2 else 1
        for p in range(3):
            received(hb[p].at[j], rs_r.at[p, j])
            whole = plane_row(fp[p].at[k], p, j)[...] + hb[p][j].astype(F32)
            plane_row(s[p].at[k], p, j)[...] = whole.astype(BF16)
            send_term_row(p, k, j)

    def own_terms():
        for p in range(3):
            own[p][...] = term(p, 0)

    def sum_c(p):
        a, b, c = PARTS[p]
        received(rb[p], rs_r.at[p, 4])
        for j in range(4):
            mine_row = plane_row(own[p], p, j)
            mine_row[...] = mine_row[...] + rb[p][0, j].astype(F32) + rb[p][1, j].astype(F32)
        r2a[p][...] = own[p][...].astype(BF16)
        for k, off in enumerate(OFFS):
            src = plane_row(r2a[p], p, REL.index(off))
            send(src, r2b[p].at[k], rs_s.at[p, 0], rs_r.at[p, 5], peer(b, off))

    def sum_b():
        for p in range(3):
            a, b, c = PARTS[p]
            received(r2b[p], rs_r.at[p, 5])
            r2s[p][...] = (
                plane_row(own[p], p, 0)[...]
                + r2b[p][0].astype(F32) + r2b[p][1].astype(F32) + r2b[p][2].astype(F32)
            )
            for k, off in enumerate(OFFS):
                send(r2s[p].at[REL.index(off)], r3b[p].at[k], rs_s.at[p, 1], rs_r.at[p, 6], peer(a, off))

    def sum_a():
        for p in range(3):
            a, b, c = PARTS[p]
            received(r3b[p], rs_r.at[p, 6])
            dgrad[:, cols(p)] = r2s[p][0] + r3b[p][0] + r3b[p][1] + r3b[p][2]

    far_terms()
    near_terms(0)
    near_terms(1)
    away()
    pass_on(0)
    pass_on(2)
    pass_on(1)
    pass_on(3)
    weight_terms()
    w_send_rows()
    own_terms()
    w_sum_c()
    sum_c(0)
    w_sum_b()
    sum_c(1)
    w_sum_a()
    sum_c(2)
    w_take_b()
    sum_b()
    w_take_c()
    put_own(0)
    put_own(1)
    put_own(2)
    put_sibling(0)
    sum_a()
    put_sibling(1)
    put_sibling(2)
    w_take_far()
    put_own(3)
    put_sibling(3)

    flat_tab = tab.reshape(64, 32, 1024)
    for p in range(3):
        received(flat_tab.at[pl.ds(0, 63), :, cols(p)], ag_s.at[p])
        received(flat_tab.at[pl.ds(0, 60), :, cols(p)], rs_s.at[p, 0])
        received(r3b[p], rs_s.at[p, 1])
        received(w1b[p], wt_s.at[p, 0])
        received(wout.at[pl.ds(0, 192), cols(p)], wt_s.at[p, 1])
        received(wout.at[pl.ds(0, 480), cols(p)], wt_s.at[p, 2])
    for n, ref in enumerate((vis.at[mine], lab.at[mine], coded.at[mine], cg_out)):
        received(ref, d2d_s.at[n])
    received(wout, out_s.at[0])


def write_out(dgrad, wgrad, dgrad_out, wgrad_out, sem):
    copies = [pltpu.make_async_copy(dgrad, dgrad_out, sem.at[0]), pltpu.make_async_copy(wgrad, wgrad_out, sem.at[1])]
    for copy in copies:
        copy.start()
    for copy in copies:
        copy.wait()


def per_part(make):
    return [make(width) for _, width in COLS]


def local(visits, enc_weight, drug_table, labels, drug_order):
    vmem = pltpu.VMEM
    scratch = [
        vmem((1024, 1024), BF16), vmem((1024, 1024), BF16), vmem((1024, 512), BF16), vmem((512, 1024), BF16),
        vmem((32, 128), jnp.int32), vmem((32, 512), jnp.int32), vmem((128, 32), F32),
        vmem((4, 4, 4, 32, 128), BF16), vmem((1024, 128), BF16), vmem((1024, 1024), BF16), vmem((512, 1024), F32),
        vmem((4, 4, 4, 32, 1024), BF16), vmem((1024, 2048), BF16), vmem((4, 4, 4, 32, 1024), BF16),
        vmem((512, 1024), BF16), vmem((512, 1024), BF16), vmem((512, 1024), F32), vmem((512, 1024), BF16),
        *per_part(lambda n: vmem((3, 4, 4, 32, n), BF16)),
        *per_part(lambda n: vmem((2, 4, 4, 32, n), F32)),
        *per_part(lambda n: vmem((4, 4, 32, n), F32)),
        *per_part(lambda n: vmem((4, 4, 32, n), BF16)),
        *per_part(lambda n: vmem((2, 4, 4, 32, n), BF16)),
        *per_part(lambda n: vmem((4, 4, 32, n), BF16)),
        *per_part(lambda n: vmem((3, 4, 32, n), BF16)),
        *per_part(lambda n: vmem((4, 32, n), F32)),
        *per_part(lambda n: vmem((3, 32, n), F32)),
        vmem((512, 1024), F32), vmem((512, 1024), BF16),
        *per_part(lambda n: vmem((4, 3, 32, n), BF16)),
        *per_part(lambda n: vmem((32, n), F32)),
        *per_part(lambda n: vmem((3, 32, n), jnp.int16)),
        *per_part(lambda n: vmem((3, 32, n), jnp.int16)),
        *per_part(lambda n: vmem((4, 32, n), jnp.int16)),
        vmem((512, 1024), jnp.int16), vmem((512, 1024), jnp.int16),
        pltpu.SemaphoreType.DMA((5,)),
        pltpu.SemaphoreType.DMA((3,)), pltpu.SemaphoreType.DMA((3, 13)),
        pltpu.SemaphoreType.DMA((3, 2)), pltpu.SemaphoreType.DMA((3, 7)),
        pltpu.SemaphoreType.DMA((3, 3)), pltpu.SemaphoreType.DMA((3, 18)),
        pltpu.SemaphoreType.DMA((4,)), pltpu.SemaphoreType.DMA((4,)), pltpu.SemaphoreType.DMA((1,)), pltpu.SemaphoreType.DMA((3, 4)),
    ]
    anywhere = pl.BlockSpec(memory_space=pl.ANY)
    drug_grad, weight_grad = pl.pallas_call(
        kernel,
        name="step",
        out_shape=(pltpu.VMEM((32, 1024), F32), pltpu.VMEM((1024, 1024), F32)),
        in_specs=[anywhere] * 5,
        out_specs=[pl.BlockSpec(memory_space=pltpu.VMEM)] * 2,
        scratch_shapes=scratch,
        compiler_params=pltpu.CompilerParams(
            collective_id=0, has_side_effects=True, vmem_limit_bytes=54 * 2**20
        ),
    )(visits, enc_weight, drug_table, labels.T, drug_order.reshape(32, 128))
    return pl.pallas_call(
        write_out,
        name="write_out",
        out_shape=(jax.ShapeDtypeStruct((32, 1024), F32), jax.ShapeDtypeStruct((1024, 1024), F32)),
        in_specs=[pl.BlockSpec(memory_space=pltpu.VMEM)] * 2,
        out_specs=[anywhere] * 2,
        scratch_shapes=[pltpu.SemaphoreType.DMA((2,))],
        compiler_params=pltpu.CompilerParams(vmem_limit_bytes=2**20),
    )(drug_grad, weight_grad)


def solution(mesh):
    return jax.shard_map(
        local,
        mesh=mesh,
        in_specs=(
            P(("group", "inner"), None),
            P(),
            P(("group", "inner"), None),
            P(("group", "inner"), None),
            P(),
        ),
        out_specs=(P(("group", "inner"), None), P()),
        check_vma=False,
    )
```

```python
import math

import jax
import jax.numpy as jnp
from jax import lax
from jax.experimental import pallas as pl
from jax.experimental.pallas import tpu as pltpu
from jax.sharding import PartitionSpec as P

MESH = pl.DeviceIdType.MESH
F32 = jnp.float32
BF16 = jnp.bfloat16
NN = (((1,), (0,)), ((), ()))
NT = (((1,), (1,)), ((), ()))

PARTS = ((0, 1, 2), (1, 2, 0), (2, 0, 1))
COLS = ((0, 384), (384, 384), (768, 256))
OFFS = (1, -1, 2)
REL = (0, 1, -1, 2)
PAIRS = (slice(0, 2), slice(2, 4))
BACK = {1: 2, -1: 1, 2: 3}


STEPS = 780.0
FLOOR = 20.0


def encode(value):
    size = jnp.maximum(jnp.abs(value), 2.0**-FLOOR)
    code = jnp.minimum(jnp.round((jnp.log2(size) + FLOOR) * STEPS), 32767.0)
    return jnp.where(value < 0.0, -code, code).astype(jnp.int32).astype(jnp.int16)


def decode(code):
    code = code.astype(jnp.int32).astype(F32)
    size = jnp.exp2(jnp.abs(code) * (1.0 / STEPS) - FLOOR)
    return jnp.where(code == 0.0, 0.0, jnp.where(code < 0.0, -size, size))


def mod4(v):
    return lax.rem(v + 8, 4)


def kernel(
    visits, weight, table, labels, order, dgrad, wgrad,
    vis, vis_t, w_half, w_t, own_order, own_labels, order_t, sel, lab, coded, squash, tab, tab_t, res,
    cg_out, cg_in, cg_own, hgrad,
    s0, s1, s2, fp0, fp1, fp2, own0, own1, own2, hb0, hb1, hb2, rb0, rb1, rb2,
    r2a0, r2a1, r2a2, r2b0, r2b1, r2b2, r2s0, r2s1, r2s2,
    r3b0, r3b1, r3b2,
    wfull, wlow, w1b0, w1b1, w1b2, wp0, wp1, wp2, wc0, wc1, wc2, w2b0, w2b1, w2b2, w3b0, w3b1, w3b2, wout, wsib,
    load_sem, ag_s, ag_r, rs_s, rs_r, wt_s, wt_r, d2d_s, d2d_r, out_s, out_r,
):
    g, i = lax.axis_index("group"), lax.axis_index("inner")
    x = (i // 8) * 2 + g // 4
    y = lax.rem(g, 4)
    z = lax.rem(i // 2, 4)
    core = lax.rem(i, 2)
    pos = (x, y, z)

    def device(px, py, pz, pc):
        return (lax.rem(px, 2) * 4 + py, (px // 2) * 8 + pz * 2 + pc)

    def peer_of(axis, off):
        moved = [mod4(v + off) if k == axis else v for k, v in enumerate(pos)]
        return device(*moved, core)

    peers = {(axis, off): peer_of(axis, off) for axis in range(3) for off in OFFS}

    def peer(axis, off):
        return peers[axis, off]

    places = {(axis, off): mod4(pos[axis] + off) if off else pos[axis] for axis in range(3) for off in REL}
    sibling = device(x, y, z, 1 - core)
    def send(src, dst, ssem, rsem, to):
        copy = pltpu.make_async_remote_copy(
            src_ref=src, dst_ref=dst, send_sem=ssem, recv_sem=rsem, device_id=to, device_id_type=MESH
        )
        copy.start()

    def received(dst, rsem):
        pltpu.make_async_copy(dst, dst, rsem).wait()

    def cols(p):
        return pl.ds(COLS[p][0], COLS[p][1])

    def row_of(buf, p, b_at, c_at, a_at=slice(None)):
        a, b, c = PARTS[p]
        at = [None, None, None]
        at[a], at[b], at[c] = a_at, b_at, c_at
        return buf.at[at[2], at[1], at[0], :, cols(p)]

    def plane_row(buf, p, b_at):
        return buf.at[:, b_at] if p == 2 else buf.at[b_at]

    mine = pl.ds(pl.multiple_of(core * 512, 512), 512)
    theirs = pl.ds(pl.multiple_of((1 - core) * 512, 512), 512)
    loads = [
        pltpu.make_async_copy(table, tab.at[0, 0, 0], load_sem.at[0]),
        pltpu.make_async_copy(weight.at[:, mine], w_half, load_sem.at[1]),
        pltpu.make_async_copy(visits, vis.at[mine], load_sem.at[2]),
        pltpu.make_async_copy(labels, own_labels, load_sem.at[3]),
        pltpu.make_async_copy(order, own_order, load_sem.at[4]),
    ]
    for load in loads:
        load.start()
    barrier = pltpu.get_barrier_semaphore()
    partners = [peer(axis, off) for axis in range(3) for off in OFFS] + [sibling]
    for partner in partners:
        pl.semaphore_signal(barrier, inc=1, device_id=partner, device_id_type=MESH)
    pl.semaphore_wait(barrier, len(partners))

    def own_block():
        for p in range(3):
            a, b, c = PARTS[p]
            block = table.at[:, cols(p)]
            for off in OFFS:
                send(block, row_of(tab, p, 0, 0, BACK[off]), ag_s.at[p], ag_r.at[p, 12], peer(a, off))
        for p in range(3):
            a, b, c = PARTS[p]
            block = table.at[:, cols(p)]
            for k, off in enumerate(OFFS):
                send(block, row_of(tab, p, BACK[off], 0, 0), ag_s.at[p], ag_r.at[p, k], peer(b, off))
            for d, off in enumerate((1, -1)):
                send(block, row_of(tab, p, 0, BACK[off], 0), ag_s.at[p], ag_r.at[p, 3 + d], peer(c, off))

    def send_row_c(p, j):
        part = slice(None) if j else slice(1, 4)
        for d, off in enumerate((1, -1)):
            to = row_of(tab, p, j, BACK[off], part)
            send(row_of(tab, p, j, 0, part), to, ag_s.at[p], ag_r.at[p, 3 + 2 * j + d], peer(PARTS[p][2], off))

    def own_row():
        loads[0].wait()
        rest = slice(1, 4)
        for p in range(3):
            received(row_of(tab, p, 0, 0, rest), ag_r.at[p, 12])
        for p in range(3):
            for k, off in enumerate(OFFS):
                to = row_of(tab, p, BACK[off], 0, rest)
                send(row_of(tab, p, 0, 0, rest), to, ag_s.at[p], ag_r.at[p, k], peer(PARTS[p][1], off))
            send_row_c(p, 0)

    def rows_of_b(steps):
        for k in steps:
            off = OFFS[k]
            for p in range(3):
                received(row_of(tab, p, BACK[off], 0), ag_r.at[p, k])
                send_row_c(p, BACK[off])

    def rows_of_c(j):
        for p in range(3):
            for d, off in enumerate((1, -1)):
                row = row_of(tab, p, j, BACK[off])
                received(row, ag_r.at[p, 3 + 2 * j + d])
                part = slice(2 * d, 2 * d + 2)
                half = row_of(tab, p, j, BACK[off], part)
                send(half, row_of(tab, p, j, 3, part), ag_s.at[p], ag_r.at[p, 11], peer(PARTS[p][2], off))

    def far_rows():
        for p in range(3):
            received(row_of(tab, p, slice(None), 3), ag_r.at[p, 11])

    def hidden_of(rows):
        hidden = lax.dot_general(w_t[...], vis[rows, :], NT, preferred_element_type=F32)
        value = jnp.tanh(hidden)
        squash[:, rows] = value
        coded[mine, rows] = value.astype(BF16)

    lane_q = lax.broadcasted_iota(jnp.int32, (32, 32), 1)
    lane_j = lax.broadcasted_iota(jnp.int32, (32, 128), 1)

    def away_by(v, at):
        return lax.rem(v + at + jnp.where(at == 2, 1, 0) - jnp.where(at == 3, 1, 0), 4)

    def select(n, _):
        bz, by, bx = away_by(z, n // 16), away_by(y, lax.rem(n // 4, 4)), away_by(x, lax.rem(n, 4))
        q = (lax.rem(bx, 2) * 4 + by) * 4 + (bx // 2) * 2 + bz // 2
        m = lax.rem(bz, 2) * 2 + core
        rows = order_t[pl.ds(pl.multiple_of(m * 32, 32), 32), :]
        ids = jnp.sum(jnp.where(lane_q == q, rows, 0.0), axis=1, keepdims=True).astype(jnp.int32)
        ids = jnp.broadcast_to(ids, (32, 128))
        picked = jnp.where(lane_j == (ids >> 7), 1.0, 0.0)
        sel[n // 16, lax.rem(n // 4, 4), lax.rem(n, 4)] = jnp.where(lane_j == 32, -(ids & 127).astype(F32), picked).astype(BF16)
        return 0

    scale = 1.0 / 256.0

    def residual_of(zs, ys, xs):
        shape = tuple(v.stop - v.start for v in (zs, ys, xs))
        count = shape[0] * shape[1] * shape[2] * 32
        rows = tab[zs, ys, xs].reshape(count, 1024)
        picks = sel[zs, ys, xs].reshape(count, 128)
        for half in range(2):
            seen = pl.ds(half * 512, 512)
            logits = lax.dot_general(rows, coded[:, seen], NN, preferred_element_type=F32)
            gap = lax.dot_general(picks, lab[seen, :], NT, preferred_element_type=F32)
            prob = 0.5 * jnp.tanh(0.5 * logits) + 0.5
            value = (prob - jnp.where(gap == 0.0, 1.0, 0.0)) * scale
            res[zs, ys, xs, :, seen] = value.astype(BF16).reshape(*shape, 32, 512)

    def turn(n):
        tab_t[:, pl.ds(n * 512, 512)] = tab[n].reshape(512, 1024).T

    near, far, all_of = slice(0, 3), slice(3, 4), slice(0, 4)

    own_block()
    send(visits, vis.at[mine], d2d_s.at[0], d2d_r.at[0], sibling)
    loads[3].wait()
    column = lax.broadcasted_iota(jnp.int32, (32, 512), 0)
    ids_in_range = (own_labels[...] - column * 128).astype(F32)
    lab[mine, :] = jnp.concatenate([ids_in_range, jnp.ones((1, 512), F32), jnp.zeros((95, 512), F32)], axis=0).T.astype(BF16)
    send(lab.at[mine], lab.at[mine], d2d_s.at[1], d2d_r.at[1], sibling)
    own_row()
    loads[1].wait()
    w_t[...] = w_half[...].T
    loads[2].wait()
    hidden_of(mine)
    rows_of_b((0, 1))
    rows_of_c(0)
    received(vis.at[theirs], d2d_r.at[0])
    hidden_of(theirs)
    send(coded.at[mine], coded.at[mine], d2d_s.at[2], d2d_r.at[2], sibling)
    rows_of_b((2,))
    loads[4].wait()
    order_t[...] = own_order[...].astype(F32).T
    lax.fori_loop(0, 64, select, 0)
    rows_of_c(1)
    vis_t[...] = vis[...].T
    rows_of_c(2)
    rows_of_c(3)
    received(coded.at[theirs], d2d_r.at[2])
    received(lab.at[theirs], d2d_r.at[1])

    for n in range(3):
        residual_of(slice(n, n + 1), near, near)
    far_rows()
    turn(3)
    residual_of(far, all_of, all_of)
    turn(0)
    turn(1)
    residual_of(near, far, all_of)
    turn(2)
    residual_of(near, near, far)

    flat = res.reshape(2048, 1024)

    def coded_grad(rows, seen):
        return lax.dot_general(tab_t[rows, :], flat[:, seen], NN, preferred_element_type=F32)

    def away():
        for n in range(2):
            seen = pl.ds(n * 512, 512)
            cg_out[:, seen] = coded_grad(theirs, seen).astype(BF16)
            send(cg_out.at[:, seen], cg_in.at[:, seen], d2d_s.at[3], d2d_r.at[3], sibling)

    s, fp, own = (s0, s1, s2), (fp0, fp1, fp2), (own0, own1, own2)
    hb, rb = (hb0, hb1, hb2), (rb0, rb1, rb2)
    r2a, r2b, r2s, r3b = (r2a0, r2a1, r2a2), (r2b0, r2b1, r2b2), (r2s0, r2s1, r2s2), (r3b0, r3b1, r3b2)

    def term(p, at):
        rows = (res[at], res[:, :, at], res[:, at])[p].reshape(512, 1024)
        value = lax.dot_general(rows, coded[cols(p), :], NT, preferred_element_type=F32)
        return value.reshape(4, 4, 32, COLS[p][1])

    def far_terms():
        for p in range(3):
            s[p][2] = term(p, 3).astype(BF16)
            for k, pair in enumerate(PAIRS):
                src = plane_row(s[p].at[2], p, pair)
                send(src, plane_row(hb[p], p, pair), rs_s.at[p, 0], rs_r.at[p, k], peer(PARTS[p][2], OFFS[k]))

    def weight_terms():
        cg_own[...] = coded_grad(mine, slice(None))
        received(cg_in, d2d_r.at[3])
        hgrad[...] = ((cg_own[...] + cg_in[...].astype(F32)) * (1.0 - squash[...] * squash[...])).astype(BF16)
        for half in range(2):
            value = lax.dot_general(vis_t[pl.ds(half * 512, 512), :], hgrad[...], NT, preferred_element_type=F32)
            wfull[:, pl.ds(half * 512, 512)] = value
            wlow[:, pl.ds(half * 512, 512)] = value.astype(BF16)

    w1b, wp, wc = (w1b0, w1b1, w1b2), (wp0, wp1, wp2), (wc0, wc1, wc2)
    w2b, w3b = (w2b0, w2b1, w2b2), (w3b0, w3b1, w3b2)

    def span(at, size):
        return pl.ds(pl.multiple_of(at * size, size), size)

    def w_row(c_at, b_at):
        return span(c_at * 4 + b_at, 32)

    def w_send_rows():
      for j in (1, 2, 3, 0):
        for k, off in enumerate(OFFS):
            for p in range(3):
                a, b, c = PARTS[p]
                src = wlow.at[w_row(places[c, off], places[b, REL[j]]), cols(p)]
                send(src, w1b[p].at[j, k], wt_s.at[p, 0], wt_r.at[p, j], peer(c, off))

    def w_sum_c():
        for j in (1, 2, 3, 0):
            for p in range(3):
                a, b, c = PARTS[p]
                received(w1b[p].at[j], wt_r.at[p, j])
                whole = (
                    wfull[w_row(pos[c], places[b, REL[j]]), cols(p)]
                    + w1b[p][j, 0].astype(F32) + w1b[p][j, 1].astype(F32) + w1b[p][j, 2].astype(F32)
                )
                if j:
                    wc[p][j - 1] = encode(whole)
                    send(wc[p].at[j - 1], w2b[p].at[j - 1], wt_s.at[p, 1], wt_r.at[p, 4], peer(b, REL[j]))
                else:
                    wp[p][...] = whole

    def w_sum_b():
        for p in range(3):
            a, b, c = PARTS[p]
            received(w2b[p], wt_r.at[p, 4])
            w3b[p][pos[a]] = encode(wp[p][...] + decode(w2b[p][0]) + decode(w2b[p][1]) + decode(w2b[p][2]))
            own_slot = w3b[p].at[pos[a]]
            for off in OFFS:
                send(own_slot, own_slot, wt_s.at[p, 1], wt_r.at[p, 5], peer(a, off))

    def w_send_c(p, j):
        a, b, c = PARTS[p]
        row = wout.at[w_row(0, places[b, REL[j]]), cols(p)]
        for d, off in enumerate((1, -1)):
            send(row, wout.at[w_row(BACK[off], places[b, REL[j]]), cols(p)], wt_s.at[p, 2], wt_r.at[p, 9 + 2 * j + d], peer(c, off))

    def w_sum_a():
        for p in range(3):
            a, b, c = PARTS[p]
            received(w3b[p].at[pl.ds(0, 3)], wt_r.at[p, 5])
            at = w_row(0, pos[b])
            wout[at, cols(p)] = encode(decode(w3b[p][0]) + decode(w3b[p][1]) + decode(w3b[p][2]) + decode(w3b[p][3]))
            row = wout.at[at, cols(p)]
            for k, off in enumerate(OFFS):
                send(row, row, wt_s.at[p, 2], wt_r.at[p, 6 + k], peer(b, off))
            w_send_c(p, 0)

    pieces = (((0, 0, 384),), ((384, 0, 128), (512, 1, 256)), ((768, 1, 256),))

    def deliver(p, at):
        src = wout.at[pl.ds(at * 128, 128), cols(p)]
        send(src, wsib.at[pl.ds(at * 128, 128), cols(p)], out_s.at[0], out_r.at[p, at], sibling)

    def put(buf, column, p, at):
        c_at = places[PARTS[p][2], REL[at]]
        for lo, half, size in pieces[p]:
            rows = pl.ds(pl.multiple_of(half * 512 + c_at * 128, 128), 128)
            lanes = pl.ds(pl.multiple_of(column * 512 + lo - half * 512, 128), size)
            wgrad[rows, lanes] = decode(buf[pl.ds(at * 128, 128), pl.ds(lo, size)])

    def put_own(at):
        for p in range(3):
            put(wout, core, p, at)

    def put_sibling(at):
        for p in range(3):
            received(wsib.at[pl.ds(at * 128, 128), cols(p)], out_r.at[p, at])
            put(wsib, 1 - core, p, at)

    def w_take_b():
        for k, off in enumerate(OFFS):
            for p in range(3):
                j = BACK[off]
                received(wout.at[w_row(0, places[PARTS[p][1], REL[j]]), cols(p)], wt_r.at[p, 6 + k])
                w_send_c(p, j)
        for p in range(3):
            deliver(p, 0)

    def w_take_c():
        for j in range(4):
            for p in range(3):
                a, b, c = PARTS[p]
                for d, off in enumerate((1, -1)):
                    row = wout.at[w_row(BACK[off], places[b, REL[j]]), cols(p)]
                    received(row, wt_r.at[p, 9 + 2 * j + d])
                    here = pl.ds(pl.multiple_of((BACK[off] * 4 + places[b, REL[j]]) * 32 + 16 * d, 16), 16)
                    there = pl.ds(pl.multiple_of((12 + places[b, REL[j]]) * 32 + 16 * d, 16), 16)
                    send(wout.at[here, cols(p)], wout.at[there, cols(p)], wt_s.at[p, 2], wt_r.at[p, 17], peer(c, off))
        for p in range(3):
            deliver(p, 1)
            deliver(p, 2)

    def w_take_far():
        for p in range(3):
            received(wout.at[pl.ds(384, 128), cols(p)], wt_r.at[p, 17])
            deliver(p, 3)

    def send_term_rows(p, k, pair):
        src = plane_row(s[p].at[k], p, pair)
        send(src, plane_row(rb[p].at[k], p, pair), rs_s.at[p, 0], rs_r.at[p, 4], peer(PARTS[p][2], OFFS[k]))

    def near_terms(k):
        for p in range(3):
            value = term(p, 1 + k)
            fp[p][k] = value
            s[p][k] = value.astype(BF16)
            send_term_rows(p, k, PAIRS[1 - k])

    def pass_on(k):
        pair = PAIRS[k]
        for p in range(3):
            received(plane_row(hb[p], p, pair), rs_r.at[p, k])
            whole = plane_row(fp[p].at[k], p, pair)[...] + plane_row(hb[p], p, pair)[...].astype(F32)
            plane_row(s[p].at[k], p, pair)[...] = whole.astype(BF16)
            send_term_rows(p, k, pair)

    def own_terms():
        for p in range(3):
            own[p][...] = term(p, 0)

    def sum_c(p):
        b = PARTS[p][1]
        received(rb[p], rs_r.at[p, 4])
        own[p][...] = own[p][...] + rb[p][0].astype(F32) + rb[p][1].astype(F32)
        r2a[p][...] = own[p][...].astype(BF16)
        for k, off in enumerate(OFFS):
            src = plane_row(r2a[p], p, REL.index(off))
            send(src, r2b[p].at[k], rs_s.at[p, 0], rs_r.at[p, 5], peer(b, off))

    def sum_b():
        for p in range(3):
            a, b, c = PARTS[p]
            received(r2b[p], rs_r.at[p, 5])
            r2s[p][...] = (
                plane_row(own[p], p, 0)[...]
                + r2b[p][0].astype(F32) + r2b[p][1].astype(F32) + r2b[p][2].astype(F32)
            )
            for k, off in enumerate(OFFS):
                send(r2s[p].at[REL.index(off)], r3b[p].at[k], rs_s.at[p, 1], rs_r.at[p, 6], peer(a, off))

    def sum_a():
        for p in range(3):
            a, b, c = PARTS[p]
            received(r3b[p], rs_r.at[p, 6])
            dgrad[:, cols(p)] = r2s[p][0] + r3b[p][0] + r3b[p][1] + r3b[p][2]

    far_terms()
    near_terms(0)
    near_terms(1)
    away()
    pass_on(0)
    pass_on(1)
    weight_terms()
    w_send_rows()
    own_terms()
    w_sum_c()
    w_sum_b()
    sum_c(0)
    sum_c(1)
    sum_c(2)
    w_sum_a()
    w_take_b()
    sum_b()
    w_take_c()
    put_own(0)
    put_own(1)
    put_own(2)
    put_sibling(0)
    sum_a()
    put_sibling(1)
    put_sibling(2)
    w_take_far()
    put_own(3)
    put_sibling(3)

    flat_tab = tab.reshape(64, 32, 1024)
    for p in range(3):
        received(flat_tab.at[pl.ds(0, 63), :, cols(p)], ag_s.at[p])
        received(flat_tab.at[pl.ds(0, 60), :, cols(p)], rs_s.at[p, 0])
        received(r3b[p], rs_s.at[p, 1])
        received(w1b[p], wt_s.at[p, 0])
        received(wout.at[pl.ds(0, 192), cols(p)], wt_s.at[p, 1])
        received(wout.at[pl.ds(0, 480), cols(p)], wt_s.at[p, 2])
    for n, ref in enumerate((vis.at[mine], lab.at[mine], coded.at[mine], cg_out)):
        received(ref, d2d_s.at[n])
    received(wout, out_s.at[0])


def write_out(dgrad, wgrad, dgrad_out, wgrad_out, sem):
    copies = [pltpu.make_async_copy(dgrad, dgrad_out, sem.at[0]), pltpu.make_async_copy(wgrad, wgrad_out, sem.at[1])]
    for copy in copies:
        copy.start()
    for copy in copies:
        copy.wait()


def per_part(make):
    return [make(width) for _, width in COLS]


def local(visits, enc_weight, drug_table, labels, drug_order):
    vmem = pltpu.VMEM
    scratch = [
        vmem((1024, 1024), BF16), vmem((1024, 1024), BF16), vmem((1024, 512), BF16), vmem((512, 1024), BF16),
        vmem((32, 128), jnp.int32), vmem((32, 512), jnp.int32), vmem((128, 32), F32),
        vmem((4, 4, 4, 32, 128), BF16), vmem((1024, 128), BF16), vmem((1024, 1024), BF16), vmem((512, 1024), F32),
        vmem((4, 4, 4, 32, 1024), BF16), vmem((1024, 2048), BF16), vmem((4, 4, 4, 32, 1024), BF16),
        vmem((512, 1024), BF16), vmem((512, 1024), BF16), vmem((512, 1024), F32), vmem((512, 1024), BF16),
        *per_part(lambda n: vmem((3, 4, 4, 32, n), BF16)),
        *per_part(lambda n: vmem((2, 4, 4, 32, n), F32)),
        *per_part(lambda n: vmem((4, 4, 32, n), F32)),
        *per_part(lambda n: vmem((4, 4, 32, n), BF16)),
        *per_part(lambda n: vmem((2, 4, 4, 32, n), BF16)),
        *per_part(lambda n: vmem((4, 4, 32, n), BF16)),
        *per_part(lambda n: vmem((3, 4, 32, n), BF16)),
        *per_part(lambda n: vmem((4, 32, n), F32)),
        *per_part(lambda n: vmem((3, 32, n), F32)),
        vmem((512, 1024), F32), vmem((512, 1024), BF16),
        *per_part(lambda n: vmem((4, 3, 32, n), BF16)),
        *per_part(lambda n: vmem((32, n), F32)),
        *per_part(lambda n: vmem((3, 32, n), jnp.int16)),
        *per_part(lambda n: vmem((3, 32, n), jnp.int16)),
        *per_part(lambda n: vmem((4, 32, n), jnp.int16)),
        vmem((512, 1024), jnp.int16), vmem((512, 1024), jnp.int16),
        pltpu.SemaphoreType.DMA((5,)),
        pltpu.SemaphoreType.DMA((3,)), pltpu.SemaphoreType.DMA((3, 13)),
        pltpu.SemaphoreType.DMA((3, 2)), pltpu.SemaphoreType.DMA((3, 7)),
        pltpu.SemaphoreType.DMA((3, 3)), pltpu.SemaphoreType.DMA((3, 18)),
        pltpu.SemaphoreType.DMA((4,)), pltpu.SemaphoreType.DMA((4,)), pltpu.SemaphoreType.DMA((1,)), pltpu.SemaphoreType.DMA((3, 4)),
    ]
    anywhere = pl.BlockSpec(memory_space=pl.ANY)
    drug_grad, weight_grad = pl.pallas_call(
        kernel,
        name="step",
        out_shape=(pltpu.VMEM((32, 1024), F32), pltpu.VMEM((1024, 1024), F32)),
        in_specs=[anywhere] * 5,
        out_specs=[pl.BlockSpec(memory_space=pltpu.VMEM)] * 2,
        scratch_shapes=scratch,
        compiler_params=pltpu.CompilerParams(
            collective_id=0, has_side_effects=True, vmem_limit_bytes=54 * 2**20
        ),
    )(visits, enc_weight, drug_table, labels.T, drug_order.reshape(32, 128))
    return pl.pallas_call(
        write_out,
        name="write_out",
        out_shape=(jax.ShapeDtypeStruct((32, 1024), F32), jax.ShapeDtypeStruct((1024, 1024), F32)),
        in_specs=[pl.BlockSpec(memory_space=pltpu.VMEM)] * 2,
        out_specs=[anywhere] * 2,
        scratch_shapes=[pltpu.SemaphoreType.DMA((2,))],
        compiler_params=pltpu.CompilerParams(vmem_limit_bytes=2**20),
    )(drug_grad, weight_grad)


def solution(mesh):
    return jax.shard_map(
        local,
        mesh=mesh,
        in_specs=(
            P(("group", "inner"), None),
            P(),
            P(("group", "inner"), None),
            P(("group", "inner"), None),
            P(),
        ),
        out_specs=(P(("group", "inner"), None), P()),
        check_vma=False,
    )
```

```python
import math

import jax
import jax.numpy as jnp
from jax import lax
from jax.experimental import pallas as pl
from jax.experimental.pallas import tpu as pltpu
from jax.sharding import PartitionSpec as P

MESH = pl.DeviceIdType.MESH
F32 = jnp.float32
BF16 = jnp.bfloat16
NN = (((1,), (0,)), ((), ()))
NT = (((1,), (1,)), ((), ()))

PARTS = ((0, 1, 2), (1, 2, 0), (2, 0, 1))
COLS = ((0, 384), (384, 384), (768, 256))
OFFS = (1, -1, 2)
REL = (0, 1, -1, 2)
PAIRS = (slice(0, 2), slice(2, 4))
BACK = {1: 2, -1: 1, 2: 3}


STEPS = 780.0
FLOOR = 20.0


def encode(value):
    size = jnp.maximum(jnp.abs(value), 2.0**-FLOOR)
    code = jnp.minimum(jnp.round((jnp.log2(size) + FLOOR) * STEPS), 32767.0)
    return jnp.where(value < 0.0, -code, code).astype(jnp.int32).astype(jnp.int16)


def decode(code):
    code = code.astype(jnp.int32).astype(F32)
    size = jnp.exp2(jnp.abs(code) * (1.0 / STEPS) - FLOOR)
    return jnp.where(code == 0.0, 0.0, jnp.where(code < 0.0, -size, size))


def mod4(v):
    return lax.rem(v + 8, 4)


def kernel(
    visits, weight, table, labels, order, dgrad, wgrad,
    vis, vis_t, w_half, w_t, own_order, own_labels, order_t, sel, lab, coded, squash, tab, tab_t, res,
    cg_out, cg_in, cg_own, hgrad,
    s0, s1, s2, fp0, fp1, fp2, own0, own1, own2, hb0, hb1, hb2, rb0, rb1, rb2,
    r2a0, r2a1, r2a2, r2b0, r2b1, r2b2, r2s0, r2s1, r2s2,
    r3b0, r3b1, r3b2,
    wfull, wlow, w1b0, w1b1, w1b2, wp0, wp1, wp2, wc0, wc1, wc2, w2b0, w2b1, w2b2, w3b0, w3b1, w3b2, wout, wsib,
    load_sem, ag_s, ag_r, rs_s, rs_r, wt_s, wt_r, d2d_s, d2d_r, out_s, out_r,
):
    g, i = lax.axis_index("group"), lax.axis_index("inner")
    x = (i // 8) * 2 + g // 4
    y = lax.rem(g, 4)
    z = lax.rem(i // 2, 4)
    core = lax.rem(i, 2)
    pos = (x, y, z)

    def device(px, py, pz, pc):
        return (lax.rem(px, 2) * 4 + py, (px // 2) * 8 + pz * 2 + pc)

    def peer_of(axis, off):
        moved = [mod4(v + off) if k == axis else v for k, v in enumerate(pos)]
        return device(*moved, core)

    peers = {(axis, off): peer_of(axis, off) for axis in range(3) for off in OFFS}

    def peer(axis, off):
        return peers[axis, off]

    places = {(axis, off): mod4(pos[axis] + off) if off else pos[axis] for axis in range(3) for off in REL}
    sibling = device(x, y, z, 1 - core)
    def send(src, dst, ssem, rsem, to):
        copy = pltpu.make_async_remote_copy(
            src_ref=src, dst_ref=dst, send_sem=ssem, recv_sem=rsem, device_id=to, device_id_type=MESH
        )
        copy.start()

    def received(dst, rsem):
        pltpu.make_async_copy(dst, dst, rsem).wait()

    def cols(p):
        return pl.ds(COLS[p][0], COLS[p][1])

    def row_of(buf, p, b_at, c_at, a_at=slice(None)):
        a, b, c = PARTS[p]
        at = [None, None, None]
        at[a], at[b], at[c] = a_at, b_at, c_at
        return buf.at[at[2], at[1], at[0], :, cols(p)]

    def plane_row(buf, p, b_at):
        return buf.at[:, b_at] if p == 2 else buf.at[b_at]

    mine = pl.ds(pl.multiple_of(core * 512, 512), 512)
    theirs = pl.ds(pl.multiple_of((1 - core) * 512, 512), 512)
    loads = [
        pltpu.make_async_copy(table, tab.at[0, 0, 0], load_sem.at[0]),
        pltpu.make_async_copy(weight.at[:, mine], w_half, load_sem.at[1]),
        pltpu.make_async_copy(visits, vis.at[mine], load_sem.at[2]),
        pltpu.make_async_copy(labels, own_labels, load_sem.at[3]),
        pltpu.make_async_copy(order, own_order, load_sem.at[4]),
    ]
    for load in loads:
        load.start()
    barrier = pltpu.get_barrier_semaphore()
    partners = [peer(axis, off) for axis in range(3) for off in OFFS] + [sibling]
    for partner in partners:
        pl.semaphore_signal(barrier, inc=1, device_id=partner, device_id_type=MESH)
    pl.semaphore_wait(barrier, len(partners))

    def own_block():
        for p in range(3):
            a, b, c = PARTS[p]
            block = table.at[:, cols(p)]
            for off in OFFS:
                send(block, row_of(tab, p, 0, 0, BACK[off]), ag_s.at[p], ag_r.at[p, 12], peer(a, off))
        for p in range(3):
            a, b, c = PARTS[p]
            block = table.at[:, cols(p)]
            for k, off in enumerate(OFFS):
                send(block, row_of(tab, p, BACK[off], 0, 0), ag_s.at[p], ag_r.at[p, k], peer(b, off))
            for d, off in enumerate((1, -1)):
                send(block, row_of(tab, p, 0, BACK[off], 0), ag_s.at[p], ag_r.at[p, 3 + d], peer(c, off))

    def send_row_c(p, j):
        part = slice(None) if j else slice(1, 4)
        for d, off in enumerate((1, -1)):
            to = row_of(tab, p, j, BACK[off], part)
            send(row_of(tab, p, j, 0, part), to, ag_s.at[p], ag_r.at[p, 3 + 2 * j + d], peer(PARTS[p][2], off))

    def own_row():
        loads[0].wait()
        rest = slice(1, 4)
        for p in range(3):
            received(row_of(tab, p, 0, 0, rest), ag_r.at[p, 12])
        for p in range(3):
            for k, off in enumerate(OFFS):
                to = row_of(tab, p, BACK[off], 0, rest)
                send(row_of(tab, p, 0, 0, rest), to, ag_s.at[p], ag_r.at[p, k], peer(PARTS[p][1], off))
            send_row_c(p, 0)

    def rows_of_b(steps):
        for k in steps:
            off = OFFS[k]
            for p in range(3):
                received(row_of(tab, p, BACK[off], 0), ag_r.at[p, k])
                send_row_c(p, BACK[off])

    def rows_of_c(j):
        for p in range(3):
            for d, off in enumerate((1, -1)):
                row = row_of(tab, p, j, BACK[off])
                received(row, ag_r.at[p, 3 + 2 * j + d])
                part = slice(2 * d, 2 * d + 2)
                half = row_of(tab, p, j, BACK[off], part)
                send(half, row_of(tab, p, j, 3, part), ag_s.at[p], ag_r.at[p, 11], peer(PARTS[p][2], off))

    def far_rows():
        for p in range(3):
            received(row_of(tab, p, slice(None), 3), ag_r.at[p, 11])

    def hidden_of(rows):
        hidden = lax.dot_general(w_t[...], vis[rows, :], NT, preferred_element_type=F32)
        value = jnp.tanh(hidden)
        squash[:, rows] = value
        coded[mine, rows] = value.astype(BF16)

    lane_q = lax.broadcasted_iota(jnp.int32, (32, 32), 1)
    lane_j = lax.broadcasted_iota(jnp.int32, (32, 128), 1)

    def away_by(v, at):
        return lax.rem(v + at + jnp.where(at == 2, 1, 0) - jnp.where(at == 3, 1, 0), 4)

    def select(n, _):
        bz, by, bx = away_by(z, n // 16), away_by(y, lax.rem(n // 4, 4)), away_by(x, lax.rem(n, 4))
        q = (lax.rem(bx, 2) * 4 + by) * 4 + (bx // 2) * 2 + bz // 2
        m = lax.rem(bz, 2) * 2 + core
        rows = order_t[pl.ds(pl.multiple_of(m * 32, 32), 32), :]
        ids = jnp.sum(jnp.where(lane_q == q, rows, 0.0), axis=1, keepdims=True).astype(jnp.int32)
        ids = jnp.broadcast_to(ids, (32, 128))
        picked = jnp.where(lane_j == (ids >> 7), 1.0, 0.0)
        sel[n // 16, lax.rem(n // 4, 4), lax.rem(n, 4)] = jnp.where(lane_j == 32, -(ids & 127).astype(F32), picked).astype(BF16)
        return 0

    scale = 1.0 / 256.0

    def residual_of(zs, ys, xs):
        shape = tuple(v.stop - v.start for v in (zs, ys, xs))
        count = shape[0] * shape[1] * shape[2] * 32
        rows = tab[zs, ys, xs].reshape(count, 1024)
        picks = sel[zs, ys, xs].reshape(count, 128)
        for half in range(2):
            seen = pl.ds(half * 512, 512)
            logits = lax.dot_general(rows, coded[:, seen], NN, preferred_element_type=F32)
            gap = lax.dot_general(picks, lab[seen, :], NT, preferred_element_type=F32)
            prob = 0.5 * jnp.tanh(0.5 * logits) + 0.5
            value = (prob - jnp.where(gap == 0.0, 1.0, 0.0)) * scale
            res[zs, ys, xs, :, seen] = value.astype(BF16).reshape(*shape, 32, 512)

    def turn(n):
        tab_t[:, pl.ds(n * 512, 512)] = tab[n].reshape(512, 1024).T

    near, far, all_of = slice(0, 3), slice(3, 4), slice(0, 4)

    own_block()
    send(visits, vis.at[mine], d2d_s.at[0], d2d_r.at[0], sibling)
    loads[3].wait()
    column = lax.broadcasted_iota(jnp.int32, (32, 512), 0)
    ids_in_range = (own_labels[...] - column * 128).astype(F32)
    lab[mine, :] = jnp.concatenate([ids_in_range, jnp.ones((1, 512), F32), jnp.zeros((95, 512), F32)], axis=0).T.astype(BF16)
    send(lab.at[mine], lab.at[mine], d2d_s.at[1], d2d_r.at[1], sibling)
    own_row()
    loads[1].wait()
    w_t[...] = w_half[...].T
    loads[2].wait()
    hidden_of(mine)
    rows_of_b((0, 1))
    rows_of_c(0)
    received(vis.at[theirs], d2d_r.at[0])
    hidden_of(theirs)
    send(coded.at[mine], coded.at[mine], d2d_s.at[2], d2d_r.at[2], sibling)
    rows_of_b((2,))
    loads[4].wait()
    order_t[...] = own_order[...].astype(F32).T
    lax.fori_loop(0, 64, select, 0)
    rows_of_c(1)
    vis_t[...] = vis[...].T
    rows_of_c(2)
    rows_of_c(3)
    received(coded.at[theirs], d2d_r.at[2])
    received(lab.at[theirs], d2d_r.at[1])

    for n in range(3):
        residual_of(slice(n, n + 1), near, near)
    far_rows()
    turn(3)
    residual_of(far, all_of, all_of)
    turn(0)
    turn(1)
    residual_of(near, far, all_of)
    turn(2)
    residual_of(near, near, far)

    flat = res.reshape(2048, 1024)

    def coded_grad(rows, seen):
        return lax.dot_general(tab_t[rows, :], flat[:, seen], NN, preferred_element_type=F32)

    def away():
        for n in range(2):
            seen = pl.ds(n * 512, 512)
            cg_out[:, seen] = coded_grad(theirs, seen).astype(BF16)
            send(cg_out.at[:, seen], cg_in.at[:, seen], d2d_s.at[3], d2d_r.at[3], sibling)

    s, fp, own = (s0, s1, s2), (fp0, fp1, fp2), (own0, own1, own2)
    hb, rb = (hb0, hb1, hb2), (rb0, rb1, rb2)
    r2a, r2b, r2s, r3b = (r2a0, r2a1, r2a2), (r2b0, r2b1, r2b2), (r2s0, r2s1, r2s2), (r3b0, r3b1, r3b2)

    def term(p, at):
        rows = (res[at], res[:, :, at], res[:, at])[p].reshape(512, 1024)
        value = lax.dot_general(rows, coded[cols(p), :], NT, preferred_element_type=F32)
        return value.reshape(4, 4, 32, COLS[p][1])

    def far_terms():
        for p in range(3):
            s[p][2] = term(p, 3).astype(BF16)
            for k, pair in enumerate(PAIRS):
                src = plane_row(s[p].at[2], p, pair)
                send(src, plane_row(hb[p], p, pair), rs_s.at[p, 0], rs_r.at[p, k], peer(PARTS[p][2], OFFS[k]))

    def weight_terms():
        cg_own[...] = coded_grad(mine, slice(None))
        received(cg_in, d2d_r.at[3])
        hgrad[...] = ((cg_own[...] + cg_in[...].astype(F32)) * (1.0 - squash[...] * squash[...])).astype(BF16)
        for half in range(2):
            value = lax.dot_general(vis_t[pl.ds(half * 512, 512), :], hgrad[...], NT, preferred_element_type=F32)
            wfull[:, pl.ds(half * 512, 512)] = value
            wlow[:, pl.ds(half * 512, 512)] = value.astype(BF16)
            w_send_rows((1, 2) if half else (0,))

    w1b, wp, wc = (w1b0, w1b1, w1b2), (wp0, wp1, wp2), (wc0, wc1, wc2)
    w2b, w3b = (w2b0, w2b1, w2b2), (w3b0, w3b1, w3b2)

    def span(at, size):
        return pl.ds(pl.multiple_of(at * size, size), size)

    def w_row(c_at, b_at):
        return span(c_at * 4 + b_at, 32)

    def w_send_rows(parts):
        for j in (1, 2, 3, 0):
            for k, off in enumerate(OFFS):
                for p in parts:
                    a, b, c = PARTS[p]
                    src = wlow.at[w_row(places[c, off], places[b, REL[j]]), cols(p)]
                    send(src, w1b[p].at[j, k], wt_s.at[p, 0], wt_r.at[p, j], peer(c, off))

    def w_sum_c():
        for j in (1, 2, 3, 0):
            for p in range(3):
                a, b, c = PARTS[p]
                received(w1b[p].at[j], wt_r.at[p, j])
                whole = (
                    wfull[w_row(pos[c], places[b, REL[j]]), cols(p)]
                    + w1b[p][j, 0].astype(F32) + w1b[p][j, 1].astype(F32) + w1b[p][j, 2].astype(F32)
                )
                if j:
                    wc[p][j - 1] = encode(whole)
                    send(wc[p].at[j - 1], w2b[p].at[j - 1], wt_s.at[p, 1], wt_r.at[p, 4], peer(b, REL[j]))
                else:
                    wp[p][...] = whole

    def w_sum_b():
        for p in range(3):
            a, b, c = PARTS[p]
            received(w2b[p], wt_r.at[p, 4])
            w3b[p][pos[a]] = encode(wp[p][...] + decode(w2b[p][0]) + decode(w2b[p][1]) + decode(w2b[p][2]))
            own_slot = w3b[p].at[pos[a]]
            for off in OFFS:
                send(own_slot, own_slot, wt_s.at[p, 1], wt_r.at[p, 5], peer(a, off))

    def w_send_c(p, j):
        a, b, c = PARTS[p]
        row = wout.at[w_row(0, places[b, REL[j]]), cols(p)]
        for d, off in enumerate((1, -1)):
            send(row, wout.at[w_row(BACK[off], places[b, REL[j]]), cols(p)], wt_s.at[p, 2], wt_r.at[p, 9 + 2 * j + d], peer(c, off))

    def w_sum_a():
        for p in range(3):
            a, b, c = PARTS[p]
            received(w3b[p].at[pl.ds(0, 3)], wt_r.at[p, 5])
            at = w_row(0, pos[b])
            wout[at, cols(p)] = encode(decode(w3b[p][0]) + decode(w3b[p][1]) + decode(w3b[p][2]) + decode(w3b[p][3]))
            row = wout.at[at, cols(p)]
            for k, off in enumerate(OFFS):
                send(row, row, wt_s.at[p, 2], wt_r.at[p, 6 + k], peer(b, off))
            w_send_c(p, 0)

    pieces = (((0, 0, 384),), ((384, 0, 128), (512, 1, 256)), ((768, 1, 256),))

    def deliver(p, at):
        src = wout.at[pl.ds(at * 128, 128), cols(p)]
        send(src, wsib.at[pl.ds(at * 128, 128), cols(p)], out_s.at[0], out_r.at[p, at], sibling)

    def put(buf, column, p, at):
        c_at = places[PARTS[p][2], REL[at]]
        for lo, half, size in pieces[p]:
            rows = pl.ds(pl.multiple_of(half * 512 + c_at * 128, 128), 128)
            lanes = pl.ds(pl.multiple_of(column * 512 + lo - half * 512, 128), size)
            wgrad[rows, lanes] = decode(buf[pl.ds(at * 128, 128), pl.ds(lo, size)])

    def put_own(at):
        for p in range(3):
            put(wout, core, p, at)

    def put_sibling(at):
        for p in range(3):
            received(wsib.at[pl.ds(at * 128, 128), cols(p)], out_r.at[p, at])
            put(wsib, 1 - core, p, at)

    def w_take_b():
        for k, off in enumerate(OFFS):
            for p in range(3):
                j = BACK[off]
                received(wout.at[w_row(0, places[PARTS[p][1], REL[j]]), cols(p)], wt_r.at[p, 6 + k])
                w_send_c(p, j)
        for p in range(3):
            deliver(p, 0)

    def w_take_c():
        for j in range(4):
            for p in range(3):
                a, b, c = PARTS[p]
                for d, off in enumerate((1, -1)):
                    row = wout.at[w_row(BACK[off], places[b, REL[j]]), cols(p)]
                    received(row, wt_r.at[p, 9 + 2 * j + d])
                    here = pl.ds(pl.multiple_of((BACK[off] * 4 + places[b, REL[j]]) * 32 + 16 * d, 16), 16)
                    there = pl.ds(pl.multiple_of((12 + places[b, REL[j]]) * 32 + 16 * d, 16), 16)
                    send(wout.at[here, cols(p)], wout.at[there, cols(p)], wt_s.at[p, 2], wt_r.at[p, 17], peer(c, off))
        for p in range(3):
            deliver(p, 1)
            deliver(p, 2)

    def w_take_far():
        for p in range(3):
            received(wout.at[pl.ds(384, 128), cols(p)], wt_r.at[p, 17])
            deliver(p, 3)

    def send_term_rows(p, k, pair):
        src = plane_row(s[p].at[k], p, pair)
        send(src, plane_row(rb[p].at[k], p, pair), rs_s.at[p, 0], rs_r.at[p, 4], peer(PARTS[p][2], OFFS[k]))

    def near_terms(k):
        for p in range(3):
            value = term(p, 1 + k)
            fp[p][k] = value
            s[p][k] = value.astype(BF16)
            send_term_rows(p, k, PAIRS[1 - k])

    def pass_on(k):
        pair = PAIRS[k]
        for p in range(3):
            received(plane_row(hb[p], p, pair), rs_r.at[p, k])
            whole = plane_row(fp[p].at[k], p, pair)[...] + plane_row(hb[p], p, pair)[...].astype(F32)
            plane_row(s[p].at[k], p, pair)[...] = whole.astype(BF16)
            send_term_rows(p, k, pair)

    def own_terms():
        for p in range(3):
            own[p][...] = term(p, 0)

    def sum_c(p):
        b = PARTS[p][1]
        received(rb[p], rs_r.at[p, 4])
        own[p][...] = own[p][...] + rb[p][0].astype(F32) + rb[p][1].astype(F32)
        r2a[p][...] = own[p][...].astype(BF16)
        for k, off in enumerate(OFFS):
            src = plane_row(r2a[p], p, REL.index(off))
            send(src, r2b[p].at[k], rs_s.at[p, 0], rs_r.at[p, 5], peer(b, off))

    def sum_b():
        for p in range(3):
            a, b, c = PARTS[p]
            received(r2b[p], rs_r.at[p, 5])
            r2s[p][...] = (
                plane_row(own[p], p, 0)[...]
                + r2b[p][0].astype(F32) + r2b[p][1].astype(F32) + r2b[p][2].astype(F32)
            )
            for k, off in enumerate(OFFS):
                send(r2s[p].at[REL.index(off)], r3b[p].at[k], rs_s.at[p, 1], rs_r.at[p, 6], peer(a, off))

    def sum_a():
        for p in range(3):
            a, b, c = PARTS[p]
            received(r3b[p], rs_r.at[p, 6])
            dgrad[:, cols(p)] = r2s[p][0] + r3b[p][0] + r3b[p][1] + r3b[p][2]

    far_terms()
    near_terms(0)
    near_terms(1)
    away()
    pass_on(0)
    pass_on(1)
    weight_terms()
    own_terms()
    w_sum_c()
    w_sum_b()
    sum_c(0)
    sum_c(1)
    sum_c(2)
    w_sum_a()
    w_take_b()
    sum_b()
    w_take_c()
    put_own(0)
    put_own(1)
    put_own(2)
    put_sibling(0)
    sum_a()
    put_sibling(1)
    put_sibling(2)
    w_take_far()
    put_own(3)
    put_sibling(3)

    flat_tab = tab.reshape(64, 32, 1024)
    for p in range(3):
        received(flat_tab.at[pl.ds(0, 63), :, cols(p)], ag_s.at[p])
        received(flat_tab.at[pl.ds(0, 60), :, cols(p)], rs_s.at[p, 0])
        received(r3b[p], rs_s.at[p, 1])
        received(w1b[p], wt_s.at[p, 0])
        received(wout.at[pl.ds(0, 192), cols(p)], wt_s.at[p, 1])
        received(wout.at[pl.ds(0, 480), cols(p)], wt_s.at[p, 2])
    for n, ref in enumerate((vis.at[mine], lab.at[mine], coded.at[mine], cg_out)):
        received(ref, d2d_s.at[n])
    received(wout, out_s.at[0])


def write_out(dgrad, wgrad, dgrad_out, wgrad_out, sem):
    copies = [pltpu.make_async_copy(dgrad, dgrad_out, sem.at[0]), pltpu.make_async_copy(wgrad, wgrad_out, sem.at[1])]
    for copy in copies:
        copy.start()
    for copy in copies:
        copy.wait()


def per_part(make):
    return [make(width) for _, width in COLS]


def local(visits, enc_weight, drug_table, labels, drug_order):
    vmem = pltpu.VMEM
    scratch = [
        vmem((1024, 1024), BF16), vmem((1024, 1024), BF16), vmem((1024, 512), BF16), vmem((512, 1024), BF16),
        vmem((32, 128), jnp.int32), vmem((32, 512), jnp.int32), vmem((128, 32), F32),
        vmem((4, 4, 4, 32, 128), BF16), vmem((1024, 128), BF16), vmem((1024, 1024), BF16), vmem((512, 1024), F32),
        vmem((4, 4, 4, 32, 1024), BF16), vmem((1024, 2048), BF16), vmem((4, 4, 4, 32, 1024), BF16),
        vmem((512, 1024), BF16), vmem((512, 1024), BF16), vmem((512, 1024), F32), vmem((512, 1024), BF16),
        *per_part(lambda n: vmem((3, 4, 4, 32, n), BF16)),
        *per_part(lambda n: vmem((2, 4, 4, 32, n), F32)),
        *per_part(lambda n: vmem((4, 4, 32, n), F32)),
        *per_part(lambda n: vmem((4, 4, 32, n), BF16)),
        *per_part(lambda n: vmem((2, 4, 4, 32, n), BF16)),
        *per_part(lambda n: vmem((4, 4, 32, n), BF16)),
        *per_part(lambda n: vmem((3, 4, 32, n), BF16)),
        *per_part(lambda n: vmem((4, 32, n), F32)),
        *per_part(lambda n: vmem((3, 32, n), F32)),
        vmem((512, 1024), F32), vmem((512, 1024), BF16),
        *per_part(lambda n: vmem((4, 3, 32, n), BF16)),
        *per_part(lambda n: vmem((32, n), F32)),
        *per_part(lambda n: vmem((3, 32, n), jnp.int16)),
        *per_part(lambda n: vmem((3, 32, n), jnp.int16)),
        *per_part(lambda n: vmem((4, 32, n), jnp.int16)),
        vmem((512, 1024), jnp.int16), vmem((512, 1024), jnp.int16),
        pltpu.SemaphoreType.DMA((5,)),
        pltpu.SemaphoreType.DMA((3,)), pltpu.SemaphoreType.DMA((3, 13)),
        pltpu.SemaphoreType.DMA((3, 2)), pltpu.SemaphoreType.DMA((3, 7)),
        pltpu.SemaphoreType.DMA((3, 3)), pltpu.SemaphoreType.DMA((3, 18)),
        pltpu.SemaphoreType.DMA((4,)), pltpu.SemaphoreType.DMA((4,)), pltpu.SemaphoreType.DMA((1,)), pltpu.SemaphoreType.DMA((3, 4)),
    ]
    anywhere = pl.BlockSpec(memory_space=pl.ANY)
    drug_grad, weight_grad = pl.pallas_call(
        kernel,
        name="step",
        out_shape=(pltpu.VMEM((32, 1024), F32), pltpu.VMEM((1024, 1024), F32)),
        in_specs=[anywhere] * 5,
        out_specs=[pl.BlockSpec(memory_space=pltpu.VMEM)] * 2,
        scratch_shapes=scratch,
        compiler_params=pltpu.CompilerParams(
            collective_id=0, has_side_effects=True, vmem_limit_bytes=54 * 2**20
        ),
    )(visits, enc_weight, drug_table, labels.T, drug_order.reshape(32, 128))
    return pl.pallas_call(
        write_out,
        name="write_out",
        out_shape=(jax.ShapeDtypeStruct((32, 1024), F32), jax.ShapeDtypeStruct((1024, 1024), F32)),
        in_specs=[pl.BlockSpec(memory_space=pltpu.VMEM)] * 2,
        out_specs=[anywhere] * 2,
        scratch_shapes=[pltpu.SemaphoreType.DMA((2,))],
        compiler_params=pltpu.CompilerParams(vmem_limit_bytes=2**20),
    )(drug_grad, weight_grad)


def solution(mesh):
    return jax.shard_map(
        local,
        mesh=mesh,
        in_specs=(
            P(("group", "inner"), None),
            P(),
            P(("group", "inner"), None),
            P(("group", "inner"), None),
            P(),
        ),
        out_specs=(P(("group", "inner"), None), P()),
        check_vma=False,
    )
```
